512 devices in a mesh: dp: 16 (over z_hi, y), tensor: 32 (over x, z_lo, core).
Axes of the slice: x: 4, y: 8, z: 8 (z_hi: 2, z_lo: 4; z = z_hi * 4 + z_lo), core: 2. Of those that a mesh axis runs over, the one named last changes fastest.
Arguments:
- inputs: bfloat16 [3072, 5120], P('dp', 'tensor'), may hold values from -6 to 6
- grad_out: bfloat16 [3072, 5120], P('dp', 'tensor'), may hold values from -6 to 6
- gate_codes: int32 [5120, 8192], P('dp', 'tensor'), may hold values from 0 to 127
- up_codes: int32 [5120, 8192], P('dp', 'tensor'), may hold values from 0 to 127
- down_codes: int32 [5120, 8192], P('dp', 'tensor'), may hold values from 0 to 127
Outputs:
- input_grad: bfloat16 [3072, 5120], P(('dp', 'tensor'))
- down_log_grad: float32 [5120, 8192], P('dp', 'tensor')
The draws below stay inside these ranges and needn't reach their ends.
Inputs may be any that keep to these rules, and one draw needn't show every extreme that they name: `gate_codes`: each word holds a sign bit (bit 0, 1 meaning negative) and a log-magnitude code (the word divided by 2). `up_codes`: each word holds a sign bit (bit 0, 1 meaning negative) and a log-magnitude code (the word divided by 2). `down_codes`: each word holds a sign bit (bit 0, 1 meaning negative) and a log-magnitude code (the word divided by 2).
All inputs are finite; a program needn't handle non-finite values.
Results may differ from the reference program's by a relative error of at most 0.024.
Values may be sent and summed in bfloat16 or wider, within the bound.
No kernel may reach another device: no remote copies, remote signals or barrier semaphores. Data moves between devices by JAX's collectives and lax.ppermute only.
A program may use at most 64 MiB of HBM per device.

```python
import math
import jax
import jax.numpy as jnp
from jax import lax

D = 5120
FF_W = 8192
TOK_DEV = 192
TOKENS = 3072
N_DP = 16
N_TENSOR = 32


def touch_ends(entries, own_key, low, largest):
    longest = entries.shape.index(max(entries.shape))
    spots = []
    for shift in (0, 1):
        where = [jax.random.randint(jax.random.fold_in(own_key, axis), (), 0, length) for axis, length in enumerate(entries.shape)]
        where[longest] = (where[longest] + shift) % entries.shape[longest]
        spots.append(tuple(where))
    return entries.at[spots[0]].set(low).at[spots[1]].set(largest)


def raised(array, stream_key, source, target, shards_of, factor):
    def block_of(axis_at):
        return (jnp.arange(array.shape[axis_at]) // (array.shape[axis_at] // shards_of)).reshape((-1,) + (1,) * (array.ndim - 1 - axis_at))

    first = jax.random.permutation(stream_key, shards_of)[block_of(target)]
    second = (block_of(target) + shards_of // 2) % shards_of
    return jnp.where((block_of(source) == first) | (block_of(source) == second), factor * array, array)


def shard_levels(stream_key, extent, shards, least, top_value):
    loudness = 1.0
    for dim, parts in shards:
        steps = jax.random.uniform(jax.random.fold_in(jax.random.fold_in(stream_key, 6), dim), (parts,), jnp.float32, least / len(shards), top_value / len(shards))
        loudness = loudness * jnp.repeat(jnp.exp(steps), extent[dim] // parts).reshape((-1,) + (1,) * (len(extent) - 1 - dim))
    return loudness


def bell_draw(own_key, extent, deviation, most, pieces=(), kind=jnp.bfloat16):
    gain = shard_levels(own_key, extent, pieces, -0.22, 0.18) if pieces else 1.0
    values = jax.random.normal(own_key, extent, jnp.float32) * deviation * gain
    return jnp.minimum(jnp.maximum(values, -most), most).astype(kind)


def noise_with(key, shape, width, bound, pieces, heavy, kind=jnp.bfloat16):
    values = width * jax.random.normal(key, shape, jnp.float32)
    if pieces:
        values = values * shard_levels(key, shape, pieces, -0.22, 0.18)
    return jnp.clip(raised(values, jax.random.fold_in(key, 3), *heavy), -bound, bound).astype(kind)


def setup_inputs(seed: int = 0) -> dict:
    streams_of = jax.random.split(jax.random.key(seed), 6)
    return {
        "inputs": bell_draw(streams_of[0], (TOKENS, D), 1.0, 6.0, ((0, 16), (1, 32))),
        "grad_out": noise_with(streams_of[1], (TOKENS, D), 1.0, 6.0, ((0, 16), (1, 32)), (0, 1, 32, 2.75)),
        "gate_codes": touch_ends(jax.random.randint(streams_of[2], (D, FF_W), 0, 128), jax.random.fold_in(streams_of[2], 1), 0, 127).astype(jnp.int32),
        "up_codes": touch_ends(jax.random.randint(streams_of[3], (D, FF_W), 0, 128), jax.random.fold_in(streams_of[3], 1), 0, 127).astype(jnp.int32),
        "down_codes": touch_ends(jax.random.randint(streams_of[4], (D, FF_W), 0, 128), jax.random.fold_in(streams_of[4], 1), 0, 127).astype(jnp.int32),
    }


coef_one = 0.6931472
coef_two = 0.2402265
coef_three = 0.0555041

def decode(packed, fan):
    sign_bit = packed % 2
    level = packed // 2
    whole = level // 8
    frac = (level % 8).astype(jnp.float32) / 8.0
    power = jnp.where(whole % 2 == 1, 0.5, 1.0).astype(jnp.float32)
    power = power * jnp.where(whole // 2 % 2 == 1, 0.25, 1.0).astype(jnp.float32)
    power = power * jnp.where(whole // 4 % 2 == 1, 0.0625, 1.0).astype(jnp.float32)
    poly = 1.0 - frac * (coef_one - frac * (coef_two - coef_three * frac))
    factor = 1.0 - 2.0 * sign_bit.astype(jnp.float32)
    return factor * power * poly * (3.0 / math.sqrt(fan))

def reference(inputs, grad_out, gate_codes, up_codes, down_codes):
    gate_b = decode(gate_codes, D).astype(jnp.bfloat16)
    up_b = decode(up_codes, D).astype(jnp.bfloat16)
    down_w = decode(down_codes, FF_W)
    down_b = down_w.astype(jnp.bfloat16)
    gate = jnp.dot(inputs, gate_b, preferred_element_type=jnp.float32)
    up = jnp.dot(inputs, up_b, preferred_element_type=jnp.float32)
    sig = jax.nn.sigmoid(gate)
    hidden = (gate * sig * up).astype(jnp.bfloat16)
    hidden_grad = jnp.dot(grad_out, down_b, preferred_element_type=jnp.float32)
    gate_grad = (hidden_grad * up * sig * (1.0 + gate * (1.0 - sig))).astype(jnp.bfloat16)
    up_grad = (hidden_grad * gate * sig).astype(jnp.bfloat16)
    hid_block = FF_W // N_TENSOR
    dims = (((1,), (1,)), ((), ()))

    def input_step(total, index):
        start = (index * hid_block).astype(jnp.int32)
        g_cols = lax.dynamic_slice_in_dim(gate_grad, start, hid_block, 1)
        u_cols = lax.dynamic_slice_in_dim(up_grad, start, hid_block, 1)
        gw_cols = lax.dynamic_slice_in_dim(gate_b, start, hid_block, 1)
        uw_cols = lax.dynamic_slice_in_dim(up_b, start, hid_block, 1)
        partial_value = lax.dot_general(g_cols, gw_cols, dims, preferred_element_type=jnp.float32)
        partial_value = partial_value + lax.dot_general(u_cols, uw_cols, dims, preferred_element_type=jnp.float32)
        rounded = lax.optimization_barrier(partial_value.astype(jnp.bfloat16))
        return (total + rounded.astype(jnp.float32), None)
    input_total, _ = lax.scan(input_step, jnp.zeros((TOKENS, D), jnp.float32), jnp.arange(N_TENSOR, dtype=jnp.int32))
    input_grad = input_total.astype(jnp.bfloat16)

    def down_step(total, index):
        start = (index * TOK_DEV).astype(jnp.int32)
        g_rows = lax.dynamic_slice_in_dim(grad_out, start, TOK_DEV, 0)
        h_rows = lax.dynamic_slice_in_dim(hidden, start, TOK_DEV, 0)
        partial_value = lax.dot_general(g_rows, h_rows, (((0,), (0,)), ((), ())), preferred_element_type=jnp.float32)
        rounded = lax.optimization_barrier(partial_value.astype(jnp.bfloat16))
        return (total + rounded.astype(jnp.float32), None)
    down_grad, _ = lax.scan(down_step, jnp.zeros((D, FF_W), jnp.float32), jnp.arange(N_DP, dtype=jnp.int32))
    return (input_grad, down_grad * down_w)
```

```python
import math

import jax
import jax.numpy as jnp
from jax import lax
from jax.experimental import pallas as pl
from jax.experimental.pallas import tpu as pltpu
from jax.sharding import PartitionSpec as P

D = 5120
FF_W = 8192
N_Z, N_Y, N_X, N_ZL = 2, 8, 4, 4
N_T = N_X * N_ZL * 2
TOK = 192
FEAT = 160
ROWS = 320
COLS = 256
HALF = D // 2

coef_one = 0.6931472
coef_two = 0.2402265
coef_three = 0.0555041

NN = (((1,), (0,)), ((), ()))
NT = (((1,), (1,)), ((), ()))


def _swap_pairs():
    pairs = []
    for z in range(N_Z):
        for y in range(N_Y):
            for t in range(N_T):
                x1, rest = t // 16, t % 16
                pairs.append(((z * N_Y + y) * N_T + t, (x1 * N_Y + y) * N_T + z * 16 + rest))
    return pairs


SWAP = _swap_pairs()
Z_SWAP = [(d, (d + N_Y) % (N_Z * N_Y)) for d in range(N_Z * N_Y)]
CORE_SWAP = [(t, t ^ 1) for t in range(N_T)]
ZC_GROUPS = [[x * 8 + i for i in range(8)] for x in range(N_X)]
X_GROUPS = [[x * 8 + i for x in range(N_X)] for i in range(8)]
Y_GROUPS = [[z * N_Y + y for y in range(N_Y)] for z in range(N_Z)]
ZXZ_GROUPS = [
    [(z * N_Y + y) * N_T + x * 8 + zl * 2 + c for z in range(N_Z) for x in range(N_X) for zl in range(N_ZL)]
    for y in range(N_Y)
    for c in range(2)
]


def decode(packed, fan):
    frac = ((packed >> 1) & 7).astype(jnp.float32) * 0.125
    power = jnp.where((packed & 16) != 0, 0.5, 1.0)
    power = power * jnp.where((packed & 32) != 0, 0.25, 1.0)
    power = power * jnp.where((packed & 64) != 0, 0.0625, 1.0)
    poly = 1.0 - frac * (coef_one - frac * (coef_two - coef_three * frac))
    value = power * poly * (3.0 / math.sqrt(fan))
    return jnp.where((packed & 1) != 0, -value, value)


def decode_kernel(gate_ref, up_ref, down_ref, out_ref):
    out_ref[:, 0:COLS] = decode(gate_ref[...], D).astype(jnp.bfloat16)
    out_ref[:, COLS : 2 * COLS] = decode(up_ref[...], D).astype(jnp.bfloat16)
    out_ref[:, 2 * COLS :] = decode(down_ref[...], FF_W).astype(jnp.bfloat16)


def forward_kernel(pos_ref, near_ref, far_ref, w_ref, own_ref, send_ref):
    z, core = pos_ref[0], pos_ref[1]
    for rel in range(2):
        h = z if rel == 0 else 1 - z
        gate_up = jnp.zeros((TOK, 2 * COLS), jnp.float32)
        hidden_grad = jnp.zeros((TOK, COLS), jnp.float32)
        for x0 in range(2):
            for far in range(2):
                pair = core if far == 0 else 1 - core
                acts_ref = far_ref if far else near_ref
                acts = acts_ref[2 * h + x0].T
                w = w_ref[pl.ds(x0 * 4 + 2 * pair, 2)].reshape(2 * ROWS, 3 * COLS)
                gate_up += lax.dot_general(acts[:TOK], w[:, : 2 * COLS], NN, preferred_element_type=jnp.float32)
                hidden_grad += lax.dot_general(acts[TOK:], w[:, 2 * COLS :], NN, preferred_element_type=jnp.float32)
        target = own_ref if rel == 0 else send_ref
        target[:, : 2 * COLS] = gate_up.astype(target.dtype)
        target[:, 2 * COLS :] = hidden_grad.astype(target.dtype)


def middle_kernel(own_ref, got_ref, out_ref):
    total = own_ref[...] + got_ref[...].astype(jnp.float32)
    gate, up, hidden_grad = total[:, :COLS], total[:, COLS : 2 * COLS], total[:, 2 * COLS :]
    sig = jax.nn.sigmoid(gate)
    out_ref[:, :COLS] = (hidden_grad * up * sig * (1.0 + gate * (1.0 - sig))).astype(jnp.bfloat16)
    out_ref[:, COLS : 2 * COLS] = (hidden_grad * gate * sig).astype(jnp.bfloat16)
    out_ref[:, 2 * COLS :] = (gate * sig * up).astype(jnp.bfloat16)


def down_kernel(pos_ref, near_ref, far_ref, own_ref, got_ref, out_ref):
    z, core = pos_ref[0], pos_ref[1]
    blank = jnp.zeros((TOK, COLS), jnp.bfloat16)
    hidden = jnp.concatenate([blank, own_ref[:, 2 * COLS :], blank, got_ref[:, 2 * COLS :]], axis=0)
    for x0 in range(2):
        for far in range(2):
            pair = core if far == 0 else 1 - core
            acts_ref = far_ref if far else near_ref
            acts = jnp.concatenate([acts_ref[2 * z + x0], acts_ref[2 * (1 - z) + x0]], axis=1)
            part = lax.dot_general(acts, hidden, NN, preferred_element_type=jnp.float32)
            out_ref[pl.ds(x0 * 4 + 2 * pair, 2)] = part.astype(jnp.bfloat16).reshape(2, ROWS, COLS)


def input_kernel(pos_ref, own_ref, got_ref, w_ref, keep_ref, send_ref):
    z, core = pos_ref[0], pos_ref[1]
    shape = (2 * 128, TOK)
    row = lax.broadcasted_iota(jnp.int32, shape, 0)
    col = lax.broadcasted_iota(jnp.int32, shape, 1)
    inner = row & 7
    group = (row >> 3) & 15
    side = (row >> 7) ^ core
    wanted = group * 12 + side * 6 + inner
    pick = jnp.where((wanted == col) & (inner < 6), 1.0, 0.0).astype(jnp.bfloat16)
    grads = []
    for ref in (own_ref, got_ref):
        picked = lax.dot_general(pick, ref[:, : 2 * COLS], NN, preferred_element_type=jnp.float32)
        grads.append(picked.astype(jnp.bfloat16))
    grads = jnp.concatenate(grads, axis=0)
    for q in range(4):
        w = w_ref[2 * q : 2 * q + 2].reshape(2 * ROWS, 3 * COLS)[:, : 2 * COLS]
        part = lax.dot_general(grads, w, NT, preferred_element_type=jnp.float32).astype(jnp.bfloat16)
        at = slice(q * 2 * ROWS, (q + 1) * 2 * ROWS)
        keep_ref[z, :, at] = part[0:128]
        send_ref[z, :, at] = part[128:256]
        keep_ref[1 - z, :, at] = part[256:384]
        send_ref[1 - z, :, at] = part[384:512]


VMEM = pl.BlockSpec(memory_space=pltpu.VMEM)
SMEM = pl.BlockSpec(memory_space=pltpu.SMEM)


def call(kernel, out_shapes, *args, name, flops=0):
    specs = [SMEM if a.dtype == jnp.int32 and a.ndim == 1 else VMEM for a in args]
    moved = sum(a.size * a.dtype.itemsize for a in args)
    moved += sum(o.size * o.dtype.itemsize for o in jax.tree.leaves(out_shapes))
    return pl.pallas_call(
        kernel,
        out_shape=out_shapes,
        in_specs=specs,
        out_specs=jax.tree.map(lambda _: VMEM, out_shapes),
        compiler_params=pltpu.CompilerParams(vmem_limit_bytes=48 * 2**20),
        cost_estimate=pl.CostEstimate(flops=flops, bytes_accessed=moved, transcendentals=0),
        name=name,
    )(*args)


def shaped(shape, dtype=jnp.bfloat16):
    return jax.ShapeDtypeStruct(shape, dtype)


def on_device(inputs, grad_out, gate_codes, up_codes, down_codes):
    dp, tensor = lax.axis_index("dp"), lax.axis_index("tensor")
    z, core = dp // N_Y, tensor % 2
    pos = jnp.stack([z, core]).astype(jnp.int32)

    w_own = call(decode_kernel, shaped((ROWS, 3 * COLS)), gate_codes, up_codes, down_codes, name="decode")
    w = lax.all_gather(w_own, "dp", axis=0, axis_index_groups=Y_GROUPS)

    acts = jnp.concatenate([inputs.T, grad_out.T], axis=1)
    acts = lax.ppermute(acts, ("dp", "tensor"), SWAP)
    acts = lax.all_gather(acts, "tensor", axis=0, axis_index_groups=ZC_GROUPS, tiled=True)
    mine = lax.dynamic_slice_in_dim(acts, core * 4 * FEAT, 4 * FEAT, 0)
    mine = jnp.broadcast_to(mine[None], (N_X, 4 * FEAT, 2 * TOK))
    near = lax.all_to_all(mine, "tensor", 0, 0, axis_index_groups=X_GROUPS, tiled=True)
    far = lax.ppermute(near, "tensor", CORE_SWAP)

    flops = 2 * HALF * 3 * COLS * 2 * TOK
    own, send = call(
        forward_kernel,
        (shaped((TOK, 3 * COLS), jnp.float32), shaped((TOK, 3 * COLS))),
        pos, near, far, w, name="forward", flops=flops,
    )
    got = lax.ppermute(send, "dp", Z_SWAP)
    own = call(middle_kernel, shaped((TOK, 3 * COLS)), own, got, name="middle")
    got = lax.ppermute(own, "dp", Z_SWAP)

    down = call(down_kernel, shaped((N_Y, ROWS, COLS)), pos, near, far, own, got, name="down", flops=flops // 3)
    down_grad = lax.psum_scatter(
        down.reshape(N_Y * ROWS, COLS), "dp", scatter_dimension=0, axis_index_groups=Y_GROUPS, tiled=True
    )

    keep, send = call(
        input_kernel,
        (shaped((2, 128, HALF)), shaped((2, 128, HALF))),
        pos, own, got, w, name="input", flops=2 * flops // 3,
    )
    other = lax.ppermute(send, "tensor", CORE_SWAP)
    summed = (keep.astype(jnp.float32) + other.astype(jnp.float32)).astype(jnp.bfloat16)
    parts = lax.all_to_all(
        summed.reshape(32, 8, HALF), ("dp", "tensor"), 0, 0, axis_index_groups=ZXZ_GROUPS, tiled=True
    )
    total = jnp.sum(parts.reshape(2, 16, 8, HALF).astype(jnp.float32), axis=1).astype(jnp.bfloat16)
    input_grad = jnp.concatenate([total[0, :6], total[1, :6]], axis=1)
    return input_grad, down_grad.astype(jnp.float32) * decode(down_codes, FF_W)


def solution(mesh):
    in_specs = (P("dp", "tensor"),) * 5
    out_specs = (P(("dp", "tensor"), None), P("dp", "tensor"))
    return jax.shard_map(on_device, mesh=mesh, in_specs=in_specs, out_specs=out_specs, check_vma=False)
```

```python
import math

import jax
import jax.numpy as jnp
from jax import lax
from jax.experimental import pallas as pl
from jax.experimental.pallas import tpu as pltpu
from jax.sharding import PartitionSpec as P

D = 5120
FF_W = 8192
N_Z, N_Y, N_X, N_ZL = 2, 8, 4, 4
N_T = N_X * N_ZL * 2
TOK = 192
FEAT = 160
HALF_FEAT = 80
ROWS = 320
COLS = 256
HALF = D // 2

coef_one = 0.6931472
coef_two = 0.2402265
coef_three = 0.0555041

NN = (((1,), (0,)), ((), ()))
NT = (((1,), (1,)), ((), ()))


def _swap_pairs():
    pairs = []
    for z in range(N_Z):
        for y in range(N_Y):
            for t in range(N_T):
                x1, rest = t // 16, t % 16
                pairs.append(((z * N_Y + y) * N_T + t, (x1 * N_Y + y) * N_T + z * 16 + rest))
    return pairs


SWAP = _swap_pairs()
Z_SWAP = [(d, (d + N_Y) % (N_Z * N_Y)) for d in range(N_Z * N_Y)]
CORE_SWAP = [(t, t ^ 1) for t in range(N_T)]
ZL_GROUPS = [[x * 8 + zl * 2 + c for zl in range(N_ZL)] for x in range(N_X) for c in range(2)]
X_GROUPS = [[x * 8 + i for x in range(N_X)] for i in range(8)]
Y_GROUPS = [[z * N_Y + y for y in range(N_Y)] for z in range(N_Z)]
Z_GROUPS = [
    [(z * N_Y + y) * N_T + x * 8 + zl * 2 + c for z in range(N_Z) for zl in range(N_ZL)]
    for y in range(N_Y)
    for x in range(N_X)
    for c in range(2)
]


def decode(packed, fan):
    frac = ((packed >> 1) & 7).astype(jnp.float32) * 0.125
    power = jnp.where((packed & 16) != 0, 0.5, 1.0)
    power = power * jnp.where((packed & 32) != 0, 0.25, 1.0)
    power = power * jnp.where((packed & 64) != 0, 0.0625, 1.0)
    poly = 1.0 - frac * (coef_one - frac * (coef_two - coef_three * frac))
    value = power * poly * (3.0 / math.sqrt(fan))
    return jnp.where((packed & 1) != 0, -value, value)


def decode_kernel(gate_ref, up_ref, down_ref, out_ref, down_w_ref, codes, sems):
    copies = [
        pltpu.make_async_copy(ref, codes.at[i], sems.at[i]) for i, ref in enumerate((gate_ref, up_ref, down_ref))
    ]
    for copy in copies:
        copy.start()
    for i, fan in enumerate((D, D, FF_W)):
        copies[i].wait()
        value = decode(codes[i], fan)
        out_ref[:, :, i * COLS : (i + 1) * COLS] = value.astype(jnp.bfloat16).reshape(2, FEAT, COLS)
    down_w_ref[...] = value


def forward(acts_ref, which, w_ref):
    sums = [[None, None], [None, None]]
    for x0 in range(2):
        for kind, cols in ((0, slice(0, 2 * COLS)), (1, slice(2 * COLS, 3 * COLS))):
            rows = slice(kind * HALF_FEAT, (kind + 1) * HALF_FEAT)
            acts = []
            for h in range(2):
                part = jnp.concatenate([acts_ref[2 * h + x0, zl, rows] for zl in range(N_ZL)], axis=0)
                acts.append(part.T)
            for half in range(2):
                rows = slice(half * HALF_FEAT, (half + 1) * HALF_FEAT)
                w = [w_ref[x0 * N_ZL + zl, which, rows, cols] for zl in range(N_ZL)]
                w = jnp.concatenate(w, axis=0)
                for h in range(2):
                    part = acts[h][half * TOK : (half + 1) * TOK]
                    part = lax.dot_general(part, w, NN, preferred_element_type=jnp.float32)
                    sums[h][kind] = part if sums[h][kind] is None else sums[h][kind] + part
    return sums


def near_kernel(pos_ref, acts_ref, w_ref, out_ref):
    sums = forward(acts_ref, pos_ref[1], w_ref)
    for h in range(2):
        out_ref[h, :, : 2 * COLS] = sums[h][0]
        out_ref[h, :, 2 * COLS :] = sums[h][1]


def far_kernel(pos_ref, acts_ref, w_ref, near_ref, own_ref, gate_up_ref, hidden_grad_ref):
    sums = forward(acts_ref, 1 - pos_ref[1], w_ref)
    for h in range(2):
        gate_up = sums[h][0] + near_ref[h, :, : 2 * COLS]
        hidden_grad = sums[h][1] + near_ref[h, :, 2 * COLS :]
        own_ref[h, :, : 2 * COLS] = gate_up
        own_ref[h, :, 2 * COLS :] = hidden_grad
        gate_up_ref[h] = gate_up.astype(jnp.bfloat16)
        hidden_grad_ref[h] = hidden_grad.astype(jnp.bfloat16)


def copy_kernel(w_ref, out_ref):
    out_ref[...] = w_ref[:, :, :, : 2 * COLS]


def down_kernel(pos_ref, near_ref, far_ref, own_ref, got_ref, out_ref):
    core = pos_ref[1]
    blank = jnp.zeros((TOK, COLS), jnp.bfloat16)
    rows = []
    for h in range(2):
        total = own_ref[h, :, : 2 * COLS] + got_ref[h].astype(jnp.float32)
        gate, up = total[:, :COLS], total[:, COLS:]
        hidden = (gate * jax.nn.sigmoid(gate) * up).astype(jnp.bfloat16)
        rows += [jnp.concatenate([hidden, blank], axis=1), jnp.concatenate([blank, hidden], axis=1)]
    hidden = jnp.concatenate(rows, axis=0)
    for x0 in range(2):
        for ref, which in ((near_ref, core), (far_ref, 1 - core)):
            grads = [
                jnp.concatenate([ref[2 * h + x0, zl, HALF_FEAT:] for zl in range(N_ZL)], axis=0) for h in range(2)
            ]
            acts = jnp.concatenate(grads, axis=1)
            part = lax.dot_general(acts, hidden, NN, preferred_element_type=jnp.float32).astype(jnp.bfloat16)
            for zl in range(N_ZL):
                rows = part[zl * HALF_FEAT : (zl + 1) * HALF_FEAT]
                out_ref[x0 * N_ZL + zl, which, :HALF_FEAT] = rows[:, :COLS]
                out_ref[x0 * N_ZL + zl, which, HALF_FEAT:] = rows[:, COLS:]


def input_part(pos_ref, own_ref, gate_up_ref, hidden_grad_ref, w_ref, out_ref, side):
    rows = N_X * 48
    row = lax.broadcasted_iota(jnp.int32, (rows, 2 * TOK), 0)
    col = lax.broadcasted_iota(jnp.int32, (rows, 2 * TOK), 1)
    x = (row * 1366) >> 16
    left = row - 48 * x
    h = jnp.where(left >= 24, 1, 0)
    left = left - 24 * h
    zl = (left * 10923) >> 16
    wanted = h * TOK + x * 48 + zl * 12 + side * 6 + left - 6 * zl
    pick = jnp.where(wanted == col, 1.0, 0.0).astype(jnp.bfloat16)
    grads = []
    for h in range(2):
        total = own_ref[h, :, : 2 * COLS] + gate_up_ref[h].astype(jnp.float32)
        gate, up = total[:, :COLS], total[:, COLS:]
        hidden_grad = own_ref[h, :, 2 * COLS :] + hidden_grad_ref[h].astype(jnp.float32)
        sig = jax.nn.sigmoid(gate)
        gate_grad = (hidden_grad * up * sig * (1.0 + gate * (1.0 - sig))).astype(jnp.bfloat16)
        up_grad = (hidden_grad * gate * sig).astype(jnp.bfloat16)
        grads.append(jnp.concatenate([gate_grad, up_grad], axis=1))
    grads = jnp.concatenate(grads, axis=0)
    grads = lax.dot_general(pick, grads, NN, preferred_element_type=jnp.float32).astype(jnp.bfloat16)
    for q in range(4):
        pair = w_ref[2 * q : 2 * q + 2].reshape(2 * ROWS, 2 * COLS)
        part = lax.dot_general(grads, pair, NT, preferred_element_type=jnp.float32)
        at = slice(q * 2 * ROWS, (q + 1) * 2 * ROWS)
        out_ref[:, :, at] = part.astype(jnp.bfloat16).reshape(N_X, 48, 2 * ROWS)


def input_send_kernel(pos_ref, *refs):
    input_part(pos_ref, *refs, 1 - pos_ref[1])


def input_keep_kernel(pos_ref, *refs):
    input_part(pos_ref, *refs, pos_ref[1])


def add_kernel(a_ref, b_ref, out_ref):
    out_ref[...] = (a_ref[...].astype(jnp.float32) + b_ref[...].astype(jnp.float32)).astype(jnp.bfloat16)


def x_sum_kernel(parts_ref, out_ref):
    total = parts_ref[0].astype(jnp.float32)
    for i in range(1, N_X):
        total += parts_ref[i].astype(jnp.float32)
    row = lax.broadcasted_iota(jnp.int32, (64, 48), 0)
    col = lax.broadcasted_iota(jnp.int32, (64, 48), 1)
    pick = jnp.where(((row >> 3) * 6 + (row & 7) == col) & ((row & 7) < 6), 1.0, 0.0).astype(jnp.bfloat16)
    total = lax.dot_general(pick, total.astype(jnp.bfloat16), NN, preferred_element_type=jnp.float32)
    out_ref[...] = total.astype(jnp.bfloat16)


def input_sum_kernel(parts_ref, out_ref):
    for z in range(2):
        total = parts_ref[4 * z].astype(jnp.float32)
        for i in range(1, 4):
            total += parts_ref[4 * z + i].astype(jnp.float32)
        out_ref[:, z * HALF : (z + 1) * HALF] = total[:6].astype(jnp.bfloat16)


def down_log_kernel(grad_ref, down_w_ref, out_ref):
    out_ref[...] = grad_ref[...].astype(jnp.float32) * down_w_ref[...]


VMEM = pl.BlockSpec(memory_space=pltpu.VMEM)
SMEM = pl.BlockSpec(memory_space=pltpu.SMEM)
HBM = pl.BlockSpec(memory_space=pltpu.HBM)


def call(kernel, out_shapes, *args, name, flops=0, scratch=(), hbm=(), limit=16):
    specs = [SMEM if a.dtype == jnp.int32 and a.ndim == 1 else HBM if i in hbm else VMEM for i, a in enumerate(args)]
    moved = 0
    if flops:
        moved = sum(a.size * a.dtype.itemsize for a in args)
        moved += sum(o.size * o.dtype.itemsize for o in jax.tree.leaves(out_shapes))
    return pl.pallas_call(
        kernel,
        out_shape=out_shapes,
        in_specs=specs,
        out_specs=jax.tree.map(lambda _: VMEM, out_shapes),
        scratch_shapes=scratch,
        compiler_params=pltpu.CompilerParams(vmem_limit_bytes=limit * 2**20),
        cost_estimate=pl.CostEstimate(flops=flops, bytes_accessed=moved, transcendentals=0),
        name=name,
    )(*args)


def shaped(shape, dtype=jnp.bfloat16):
    return jax.ShapeDtypeStruct(shape, dtype)


def on_device(inputs, grad_out, gate_codes, up_codes, down_codes):
    dp, tensor = lax.axis_index("dp"), lax.axis_index("tensor")
    pos = jnp.stack([dp // N_Y, tensor % 2, dp % N_Y, tensor // 2 % N_ZL]).astype(jnp.int32)
    wide, bf16, f32 = 3 * COLS, jnp.bfloat16, jnp.float32

    w, down_w = call(
        decode_kernel, (shaped((2, FEAT, wide)), shaped((ROWS, COLS), f32)), gate_codes, up_codes, down_codes,
        name="decode", flops=ROWS * COLS * 32,
        scratch=[pltpu.VMEM((3, ROWS, COLS), jnp.int32), pltpu.SemaphoreType.DMA((3,))], hbm=(0, 1, 2), limit=60,
    )
    w = lax.all_gather(w, "dp", axis=0, axis_index_groups=Y_GROUPS)

    def folded(acts):
        acts = acts.T
        return jnp.concatenate([acts[:HALF_FEAT], acts[HALF_FEAT:]], axis=1)

    acts = jnp.concatenate([folded(inputs), folded(grad_out)], axis=0)
    acts = lax.ppermute(acts, ("dp", "tensor"), SWAP)
    acts = jnp.broadcast_to(acts[None], (N_ZL, FEAT, 2 * TOK))
    acts = lax.all_to_all(acts, "tensor", 0, 0, axis_index_groups=ZL_GROUPS, tiled=True)

    acts = jnp.broadcast_to(acts[None], (N_X, N_ZL, FEAT, 2 * TOK))
    near = lax.all_to_all(acts, "tensor", 0, 0, axis_index_groups=X_GROUPS, tiled=True)
    near, w = lax.optimization_barrier((near, w))
    far = lax.ppermute(near, "tensor", CORE_SWAP)

    flops = HALF * 3 * COLS * 2 * TOK
    sums = call(near_kernel, shaped((2, TOK, wide), f32), pos, near, w, name="forward_near", flops=flops)
    own, gate_up, hidden_grad = call(
        far_kernel,
        (shaped((2, TOK, wide), f32), shaped((2, TOK, 2 * COLS)), shaped((2, TOK, COLS))),
        pos, far, w, sums, name="forward_far",
    )
    w_own, _ = lax.optimization_barrier((w, own))
    gate_up = lax.ppermute(gate_up, "dp", Z_SWAP)
    hidden_grad = lax.ppermute(hidden_grad, "dp", Z_SWAP)
    w_gate_up = call(copy_kernel, shaped((N_Y, 2, FEAT, 2 * COLS)), w_own, name="copy", flops=flops)

    down = call(down_kernel, shaped((N_Y, 2, FEAT, COLS)), pos, near, far, own, gate_up, name="down")
    down, hidden_grad, w_gate_up = lax.optimization_barrier((down, hidden_grad, w_gate_up))
    down_grad = lax.psum_scatter(
        down.reshape(N_Y * ROWS, COLS), "dp", scatter_dimension=0, axis_index_groups=Y_GROUPS, tiled=True
    )

    out = shaped((N_X, 48, HALF))
    grads = (own, gate_up, hidden_grad)
    send = call(input_send_kernel, out, pos, *grads, w_gate_up, name="input_send", flops=flops)
    other = lax.ppermute(send, "tensor", CORE_SWAP)
    keep = call(input_keep_kernel, out, pos, *grads, w_gate_up, name="input_keep", flops=flops)
    parts = call(add_kernel, out, keep, other, name="add")
    parts = lax.all_to_all(parts, "tensor", 0, 0, axis_index_groups=X_GROUPS, tiled=True)
    parts = call(x_sum_kernel, shaped((64, HALF)), parts, name="x_sum").reshape(N_Y, 8, HALF)
    parts = lax.all_to_all(parts, ("dp", "tensor"), 0, 0, axis_index_groups=Z_GROUPS, tiled=True)
    input_grad = call(input_sum_kernel, shaped((6, D)), parts, name="input_sum")
    down_log_grad = call(
        down_log_kernel, shaped((ROWS, COLS), f32), down_grad, down_w, name="down_log", flops=flops
    )
    return input_grad, down_log_grad


def solution(mesh):
    in_specs = (P("dp", "tensor"),) * 5
    out_specs = (P(("dp", "tensor"), None), P("dp", "tensor"))
    return jax.shard_map(on_device, mesh=mesh, in_specs=in_specs, out_specs=out_specs, check_vma=False)
```

```python
import math

import jax
import jax.numpy as jnp
from jax import lax
from jax.experimental import pallas as pl
from jax.experimental.pallas import tpu as pltpu
from jax.sharding import PartitionSpec as P

D = 5120
FF_W = 8192
N_Z, N_Y, N_X, N_ZL = 2, 8, 4, 4
N_T = N_X * N_ZL * 2
TOK = 192
FEAT = 160
HALF_FEAT = 80
ROWS = 320
COLS = 256
HALF = D // 2
QUARTER = HALF // 4

coef_one = 0.6931472
coef_two = 0.2402265
coef_three = 0.0555041

NN = (((1,), (0,)), ((), ()))
NT = (((1,), (1,)), ((), ()))


def _turn_pairs():
    pairs = []
    for z in range(N_Z):
        for y in range(N_Y):
            for t in range(N_T):
                x1, rest = t // 16, t % 16
                pairs.append(((z * N_Y + y) * N_T + t, (x1 * N_Y + y) * N_T + (1 - z) * 16 + rest))
    return pairs


TURN = _turn_pairs()
Z_SWAP = [(d, (d + N_Y) % (N_Z * N_Y)) for d in range(N_Z * N_Y)]
CORE_SWAP = [(t, t ^ 1) for t in range(N_T)]
ZL_GROUPS = [[x * 8 + zl * 2 + c for zl in range(N_ZL)] for x in range(N_X) for c in range(2)]
X_GROUPS = [[x * 8 + i for x in range(N_X)] for i in range(8)]
Y_GROUPS = [[z * N_Y + y for y in range(N_Y)] for z in range(N_Z)]
Z_GROUPS = [
    [(z * N_Y + y) * N_T + x * 8 + zl * 2 + c for z in range(N_Z) for zl in range(N_ZL)]
    for y in range(N_Y)
    for x in range(N_X)
    for c in range(2)
]


def decode(packed, fan):
    frac = ((packed >> 1) & 7).astype(jnp.float32) * 0.125
    power = jnp.where((packed & 16) != 0, 0.5, 1.0)
    power = power * jnp.where((packed & 32) != 0, 0.25, 1.0)
    power = power * jnp.where((packed & 64) != 0, 0.0625, 1.0)
    poly = 1.0 - frac * (coef_one - frac * (coef_two - coef_three * frac))
    value = power * poly * (3.0 / math.sqrt(fan))
    return jnp.where((packed & 1) != 0, -value, value)


def decode_kernel(gate_ref, up_ref, down_ref, out_ref, down_w_ref, codes, sems):
    copies = [
        pltpu.make_async_copy(ref, codes.at[i], sems.at[i]) for i, ref in enumerate((gate_ref, up_ref, down_ref))
    ]
    for copy in copies:
        copy.start()
    for i, fan in enumerate((D, D, FF_W)):
        copies[i].wait()
        value = decode(codes[i], fan)
        out_ref[:, :, i * COLS : (i + 1) * COLS] = value.astype(jnp.bfloat16).reshape(2, FEAT, COLS)
    down_w_ref[...] = value


def forward(acts_ref, which, w_ref):
    sums = [[None, None], [None, None]]
    for x0 in range(2):
        for kind, cols in ((0, slice(0, 2 * COLS)), (1, slice(2 * COLS, 3 * COLS))):
            rows = slice(kind * HALF_FEAT, (kind + 1) * HALF_FEAT)
            acts = []
            for h in range(2):
                part = jnp.concatenate([acts_ref[2 - 2 * h + x0, zl, rows] for zl in range(N_ZL)], axis=0)
                acts.append(part.T)
            for half in range(2):
                rows = slice(half * HALF_FEAT, (half + 1) * HALF_FEAT)
                w = [w_ref[x0 * N_ZL + zl, which, rows, cols] for zl in range(N_ZL)]
                w = jnp.concatenate(w, axis=0)
                for h in range(2):
                    part = acts[h][half * TOK : (half + 1) * TOK]
                    part = lax.dot_general(part, w, NN, preferred_element_type=jnp.float32)
                    sums[h][kind] = part if sums[h][kind] is None else sums[h][kind] + part
    return sums


def near_kernel(pos_ref, acts_ref, w_ref, out_ref):
    sums = forward(acts_ref, pos_ref[1], w_ref)
    for h in range(2):
        out_ref[h, :, : 2 * COLS] = sums[h][0]
        out_ref[h, :, 2 * COLS :] = sums[h][1]


def far_kernel(pos_ref, acts_ref, w_ref, near_ref, own_ref, gate_up_ref, hidden_grad_ref):
    sums = forward(acts_ref, 1 - pos_ref[1], w_ref)
    for h in range(2):
        gate_up = sums[h][0] + near_ref[h, :, : 2 * COLS]
        hidden_grad = sums[h][1] + near_ref[h, :, 2 * COLS :]
        own_ref[h, :, : 2 * COLS] = gate_up
        own_ref[h, :, 2 * COLS :] = hidden_grad
        gate_up_ref[h] = gate_up.astype(jnp.bfloat16)
        hidden_grad_ref[h] = hidden_grad.astype(jnp.bfloat16)


def copy_kernel(w_ref, out_ref):
    out_ref[...] = w_ref[:, :, :, : 2 * COLS]


def down_kernel(pos_ref, near_ref, far_ref, own_ref, got_ref, out_ref):
    core = pos_ref[1]
    blank = jnp.zeros((TOK, COLS), jnp.bfloat16)
    rows = []
    for h in range(2):
        total = own_ref[h, :, : 2 * COLS] + got_ref[h].astype(jnp.float32)
        gate, up = total[:, :COLS], total[:, COLS:]
        hidden = (gate * jax.nn.sigmoid(gate) * up).astype(jnp.bfloat16)
        rows += [jnp.concatenate([hidden, blank], axis=1), jnp.concatenate([blank, hidden], axis=1)]
    hidden = jnp.concatenate(rows, axis=0)
    for x0 in range(2):
        for ref, which in ((near_ref, core), (far_ref, 1 - core)):
            grads = [
                jnp.concatenate([ref[2 - 2 * h + x0, zl, HALF_FEAT:] for zl in range(N_ZL)], axis=0) for h in range(2)
            ]
            acts = jnp.concatenate(grads, axis=1)
            part = lax.dot_general(acts, hidden, NN, preferred_element_type=jnp.float32).astype(jnp.bfloat16)
            for zl in range(N_ZL):
                rows = part[zl * HALF_FEAT : (zl + 1) * HALF_FEAT]
                out_ref[x0 * N_ZL + zl, which, :HALF_FEAT] = rows[:, :COLS]
                out_ref[x0 * N_ZL + zl, which, HALF_FEAT:] = rows[:, COLS:]


def input_part(pos_ref, own_ref, gate_up_ref, hidden_grad_ref, w_ref, out_ref, side):
    rows = N_X * 48
    row = lax.broadcasted_iota(jnp.int32, (rows, 2 * TOK), 0)
    col = lax.broadcasted_iota(jnp.int32, (rows, 2 * TOK), 1)
    x = (row * 1366) >> 16
    left = row - 48 * x
    h = jnp.where(left >= 24, 1, 0)
    left = left - 24 * h
    zl = (left * 10923) >> 16
    wanted = h * TOK + x * 48 + zl * 12 + side * 6 + left - 6 * zl
    pick = jnp.where(wanted == col, 1.0, 0.0).astype(jnp.bfloat16)
    grads = []
    for h in range(2):
        total = own_ref[h, :, : 2 * COLS] + gate_up_ref[h].astype(jnp.float32)
        gate, up = total[:, :COLS], total[:, COLS:]
        hidden_grad = own_ref[h, :, 2 * COLS :] + hidden_grad_ref[h].astype(jnp.float32)
        sig = jax.nn.sigmoid(gate)
        gate_grad = (hidden_grad * up * sig * (1.0 + gate * (1.0 - sig))).astype(jnp.bfloat16)
        up_grad = (hidden_grad * gate * sig).astype(jnp.bfloat16)
        grads.append(jnp.concatenate([gate_grad, up_grad], axis=1))
    grads = jnp.concatenate(grads, axis=0)
    grads = lax.dot_general(pick, grads, NN, preferred_element_type=jnp.float32).astype(jnp.bfloat16)
    for q in range(4):
        pair = w_ref[2 * q : 2 * q + 2].reshape(2 * ROWS, 2 * COLS)
        part = lax.dot_general(grads, pair, NT, preferred_element_type=jnp.float32)
        at = slice(q * 2 * ROWS, (q + 1) * 2 * ROWS)
        out_ref[:, :, at] = part.astype(jnp.bfloat16).reshape(N_X, 48, 2 * ROWS)


def input_send_kernel(pos_ref, *refs):
    input_part(pos_ref, *refs, 1 - pos_ref[1])


def input_keep_kernel(pos_ref, *refs):
    input_part(pos_ref, *refs, pos_ref[1])


def add_kernel(a_ref, b_ref, out_ref):
    out_ref[...] = (a_ref[...].astype(jnp.float32) + b_ref[...].astype(jnp.float32)).astype(jnp.bfloat16)


def x_sum_kernel(parts_ref, out_ref):
    total = parts_ref[0].astype(jnp.float32)
    for i in range(1, N_X):
        total += parts_ref[i].astype(jnp.float32)
    total = total.astype(jnp.bfloat16)
    row = lax.broadcasted_iota(jnp.int32, (N_Y * 24, 48), 0)
    col = lax.broadcasted_iota(jnp.int32, (N_Y * 24, 48), 1)
    k = (row * 2731) >> 16
    left = row - 24 * k
    packed = None
    for q in range(4):
        inside = (left >= 6 * q) & (left < 6 * q + 6)
        pick = jnp.where(inside & (k * 6 + left - 6 * q == col), 1.0, 0.0).astype(jnp.bfloat16)
        part = total[:, q * QUARTER : (q + 1) * QUARTER]
        part = lax.dot_general(pick, part, NN, preferred_element_type=jnp.float32)
        packed = part if packed is None else packed + part
    out_ref[...] = packed.astype(jnp.bfloat16)


def input_sum_kernel(parts_ref, out_ref):
    row = lax.broadcasted_iota(jnp.int32, (8, 24), 0)
    col = lax.broadcasted_iota(jnp.int32, (8, 24), 1)
    for z in range(2):
        total = parts_ref[4 * z].astype(jnp.float32)
        for i in range(1, 4):
            total += parts_ref[4 * z + i].astype(jnp.float32)
        total = total.astype(jnp.bfloat16)
        for q in range(4):
            pick = jnp.where((row + 6 * q == col) & (row < 6), 1.0, 0.0).astype(jnp.bfloat16)
            part = lax.dot_general(pick, total, NN, preferred_element_type=jnp.float32)
            at = z * HALF + q * QUARTER
            out_ref[:, at : at + QUARTER] = part[:6].astype(jnp.bfloat16)


VMEM = pl.BlockSpec(memory_space=pltpu.VMEM)
SMEM = pl.BlockSpec(memory_space=pltpu.SMEM)
HBM = pl.BlockSpec(memory_space=pltpu.HBM)


def call(kernel, out_shapes, *args, name, flops=0, scratch=(), hbm=(), limit=16):
    specs = [SMEM if a.dtype == jnp.int32 and a.ndim == 1 else HBM if i in hbm else VMEM for i, a in enumerate(args)]
    moved = 0
    if flops:
        moved = sum(a.size * a.dtype.itemsize for a in args)
        moved += sum(o.size * o.dtype.itemsize for o in jax.tree.leaves(out_shapes))
    return pl.pallas_call(
        kernel,
        out_shape=out_shapes,
        in_specs=specs,
        out_specs=jax.tree.map(lambda _: VMEM, out_shapes),
        scratch_shapes=scratch,
        compiler_params=pltpu.CompilerParams(vmem_limit_bytes=limit * 2**20),
        cost_estimate=pl.CostEstimate(flops=flops, bytes_accessed=moved, transcendentals=0),
        name=name,
    )(*args)


def shaped(shape, dtype=jnp.bfloat16):
    return jax.ShapeDtypeStruct(shape, dtype)


def on_device(inputs, grad_out, gate_codes, up_codes, down_codes):
    dp, tensor = lax.axis_index("dp"), lax.axis_index("tensor")
    pos = jnp.stack([dp // N_Y, tensor % 2, dp % N_Y, tensor // 2 % N_ZL]).astype(jnp.int32)
    wide, bf16, f32 = 3 * COLS, jnp.bfloat16, jnp.float32

    w, down_w = call(
        decode_kernel, (shaped((2, FEAT, wide)), shaped((ROWS, COLS), f32)), gate_codes, up_codes, down_codes,
        name="decode", flops=ROWS * COLS * 32,
        scratch=[pltpu.VMEM((3, ROWS, COLS), jnp.int32), pltpu.SemaphoreType.DMA((3,))], hbm=(0, 1, 2), limit=60,
    )
    w = lax.all_gather(w, "dp", axis=0, axis_index_groups=Y_GROUPS)

    def folded(acts):
        acts = acts.T
        return jnp.concatenate([acts[:HALF_FEAT], acts[HALF_FEAT:]], axis=1)

    acts = jnp.concatenate([folded(inputs), folded(grad_out)], axis=0)
    acts = lax.ppermute(acts, ("dp", "tensor"), TURN)
    acts = jnp.broadcast_to(acts[None], (N_ZL, FEAT, 2 * TOK))
    acts = lax.all_to_all(acts, "tensor", 0, 0, axis_index_groups=ZL_GROUPS, tiled=True)

    acts = jnp.broadcast_to(acts[None], (N_X, N_ZL, FEAT, 2 * TOK))
    near = lax.all_to_all(acts, "tensor", 0, 0, axis_index_groups=X_GROUPS, tiled=True)
    near, w = lax.optimization_barrier((near, w))
    far = lax.ppermute(near, "tensor", CORE_SWAP)

    flops = HALF * 3 * COLS * 2 * TOK
    sums = call(near_kernel, shaped((2, TOK, wide), f32), pos, near, w, name="forward_near", flops=flops)
    own, gate_up, hidden_grad = call(
        far_kernel,
        (shaped((2, TOK, wide), f32), shaped((2, TOK, 2 * COLS)), shaped((2, TOK, COLS))),
        pos, far, w, sums, name="forward_far",
    )
    w_own, _ = lax.optimization_barrier((w, own))
    gate_up = lax.ppermute(gate_up, "dp", Z_SWAP)
    hidden_grad = lax.ppermute(hidden_grad, "dp", Z_SWAP)
    w_gate_up = call(copy_kernel, shaped((N_Y, 2, FEAT, 2 * COLS)), w_own, name="copy", flops=flops)

    down = call(down_kernel, shaped((N_Y, 2, FEAT, COLS)), pos, near, far, own, gate_up, name="down")
    down, hidden_grad, w_gate_up = lax.optimization_barrier((down, hidden_grad, w_gate_up))
    down_grad = lax.psum_scatter(
        down.reshape(N_Y * ROWS, COLS), "dp", scatter_dimension=0, axis_index_groups=Y_GROUPS, tiled=True
    )

    out = shaped((N_X, 48, HALF))
    grads = (own, gate_up, hidden_grad)
    send = call(input_send_kernel, out, pos, *grads, w_gate_up, name="input_send", flops=flops)
    other = lax.ppermute(send, "tensor", CORE_SWAP)
    keep = call(input_keep_kernel, out, pos, *grads, w_gate_up, name="input_keep", flops=flops)
    parts = call(add_kernel, out, keep, other, name="add")
    parts = lax.all_to_all(parts, "tensor", 0, 0, axis_index_groups=X_GROUPS, tiled=True)
    parts = call(x_sum_kernel, shaped((N_Y * 24, QUARTER)), parts, name="x_sum").reshape(N_Y, 24, QUARTER)
    parts = lax.all_to_all(parts, ("dp", "tensor"), 0, 0, axis_index_groups=Z_GROUPS, tiled=True)
    input_grad = call(input_sum_kernel, shaped((6, D)), parts, name="input_sum")
    down_log_grad = down_grad.astype(f32) * down_w
    return input_grad, down_log_grad


def solution(mesh):
    in_specs = (P("dp", "tensor"),) * 5
    out_specs = (P(("dp", "tensor"), None), P("dp", "tensor"))
    return jax.shard_map(on_device, mesh=mesh, in_specs=in_specs, out_specs=out_specs, check_vma=False)
```

```python
import functools
import math

import jax
import jax.numpy as jnp
from jax import lax
from jax.experimental import pallas as pl
from jax.experimental.pallas import tpu as pltpu
from jax.sharding import PartitionSpec as P

D = 5120
FF_W = 8192
N_Z, N_Y, N_X, N_ZL = 2, 8, 4, 4
N_T = N_X * N_ZL * 2
TOK = 192
FEAT = 160
HALF_FEAT = 80
ROWS = 320
COLS = 256
HALF = D // 2
QUARTER = HALF // 4

coef_one = 0.6931472
coef_two = 0.2402265
coef_three = 0.0555041

NN = (((1,), (0,)), ((), ()))
NT = (((1,), (1,)), ((), ()))


def _turn_pairs(step):
    pairs = []
    for z in range(N_Z):
        for y in range(N_Y):
            for t in range(N_T):
                x1, rest = t // 16, (t % 16) ^ (2 * step)
                pairs.append(((z * N_Y + y) * N_T + t, (x1 * N_Y + y) * N_T + (1 - z) * 16 + rest))
    return pairs


TURNS = [_turn_pairs(step) for step in range(N_ZL)]
Z_SWAP = [(d, (d + N_Y) % (N_Z * N_Y)) for d in range(N_Z * N_Y)]
CORE_SWAP = [(t, t ^ 1) for t in range(N_T)]
ZL_GROUPS = [[x * 8 + zl * 2 + c for zl in range(N_ZL)] for x in range(N_X) for c in range(2)]
X_GROUPS = [[x * 8 + i for x in range(N_X)] for i in range(8)]
Y_GROUPS = [[z * N_Y + y for y in range(N_Y)] for z in range(N_Z)]
Z_GROUPS = [
    [(z * N_Y + y) * N_T + x * 8 + zl * 2 + c for z in range(N_Z) for zl in range(N_ZL)]
    for y in range(N_Y)
    for x in range(N_X)
    for c in range(2)
]


def decode(packed, fan):
    frac = ((packed >> 1) & 7).astype(jnp.float32) * 0.125
    power = jnp.where((packed & 16) != 0, 0.5, 1.0)
    power = power * jnp.where((packed & 32) != 0, 0.25, 1.0)
    power = power * jnp.where((packed & 64) != 0, 0.0625, 1.0)
    poly = 1.0 - frac * (coef_one - frac * (coef_two - coef_three * frac))
    value = power * poly * (3.0 / math.sqrt(fan))
    return jnp.where((packed & 1) != 0, -value, value)


def decode_kernel(gate_ref, up_ref, down_ref, out_ref, down_w_ref, codes, sems):
    copies = [
        pltpu.make_async_copy(ref, codes.at[i], sems.at[i]) for i, ref in enumerate((gate_ref, up_ref, down_ref))
    ]
    for copy in copies:
        copy.start()
    for i, fan in enumerate((D, D, FF_W)):
        copies[i].wait()
        value = decode(codes[i], fan)
        out_ref[:, :, i * COLS : (i + 1) * COLS] = value.astype(jnp.bfloat16).reshape(2, FEAT, COLS)
    down_w_ref[...] = value


def forward(acts_ref, which, my_zl, w_ref, kind):
    cols = (slice(0, 2 * COLS), slice(2 * COLS, 3 * COLS))[kind]
    sums = [None, None]
    for x0 in range(2):
        rows = slice(kind * HALF_FEAT, (kind + 1) * HALF_FEAT)
        acts = []
        for h in range(2):
            part = jnp.concatenate([acts_ref[2 - 2 * h + x0, zl ^ my_zl, rows] for zl in range(N_ZL)], axis=0)
            acts.append(part.T)
        for half in range(2):
            rows = slice(half * HALF_FEAT, (half + 1) * HALF_FEAT)
            w = [w_ref[x0 * N_ZL + zl, which, rows, cols] for zl in range(N_ZL)]
            w = jnp.concatenate(w, axis=0)
            for h in range(2):
                part = acts[h][half * TOK : (half + 1) * TOK]
                part = lax.dot_general(part, w, NN, preferred_element_type=jnp.float32)
                sums[h] = part if sums[h] is None else sums[h] + part
    return sums


def near_kernel(pos_ref, acts_ref, w_ref, gate_up_ref, hidden_grad_ref):
    for kind, out_ref in enumerate((gate_up_ref, hidden_grad_ref)):
        for h, total in enumerate(forward(acts_ref, pos_ref[1], pos_ref[3], w_ref, kind)):
            out_ref[h] = total


def far_kernel(kind, pos_ref, acts_ref, w_ref, near_ref, own_ref, send_ref):
    for h, total in enumerate(forward(acts_ref, 1 - pos_ref[1], pos_ref[3], w_ref, kind)):
        total += near_ref[h]
        own_ref[h] = total
        send_ref[h] = total.astype(jnp.bfloat16)


def copy_kernel(w_ref, out_ref):
    out_ref[...] = w_ref[:, :, :, : 2 * COLS]


def down_kernel(pos_ref, near_ref, far_ref, own_ref, got_ref, out_ref):
    core = pos_ref[1]
    blank = jnp.zeros((TOK, COLS), jnp.bfloat16)
    rows = []
    for h in range(2):
        total = own_ref[h] + got_ref[h].astype(jnp.float32)
        gate, up = total[:, :COLS], total[:, COLS:]
        hidden = (gate * jax.nn.sigmoid(gate) * up).astype(jnp.bfloat16)
        rows += [jnp.concatenate([hidden, blank], axis=1), jnp.concatenate([blank, hidden], axis=1)]
    hidden = jnp.concatenate(rows, axis=0)
    for x0 in range(2):
        for ref, which in ((near_ref, core), (far_ref, 1 - core)):
            grads = [
                jnp.concatenate([ref[2 - 2 * h + x0, zl ^ pos_ref[3], HALF_FEAT:] for zl in range(N_ZL)], axis=0) for h in range(2)
            ]
            acts = jnp.concatenate(grads, axis=1)
            part = lax.dot_general(acts, hidden, NN, preferred_element_type=jnp.float32).astype(jnp.bfloat16)
            for zl in range(N_ZL):
                rows = part[zl * HALF_FEAT : (zl + 1) * HALF_FEAT]
                out_ref[x0 * N_ZL + zl, which, :HALF_FEAT] = rows[:, :COLS]
                out_ref[x0 * N_ZL + zl, which, HALF_FEAT:] = rows[:, COLS:]


def input_part(pos_ref, own_ref, got_ref, own_hg_ref, got_hg_ref, w_ref, out_ref, side):
    rows = N_X * 48
    row = lax.broadcasted_iota(jnp.int32, (rows, 2 * TOK), 0)
    col = lax.broadcasted_iota(jnp.int32, (rows, 2 * TOK), 1)
    x = (row * 1366) >> 16
    left = row - 48 * x
    h = jnp.where(left >= 24, 1, 0)
    left = left - 24 * h
    zl = (left * 10923) >> 16
    wanted = h * TOK + x * 48 + zl * 12 + side * 6 + left - 6 * zl
    pick = jnp.where(wanted == col, 1.0, 0.0).astype(jnp.bfloat16)
    grads = []
    for h in range(2):
        total = own_ref[h] + got_ref[h].astype(jnp.float32)
        gate, up = total[:, :COLS], total[:, COLS:]
        hidden_grad = own_hg_ref[h] + got_hg_ref[h].astype(jnp.float32)
        sig = jax.nn.sigmoid(gate)
        gate_grad = (hidden_grad * up * sig * (1.0 + gate * (1.0 - sig))).astype(jnp.bfloat16)
        up_grad = (hidden_grad * gate * sig).astype(jnp.bfloat16)
        grads.append(jnp.concatenate([gate_grad, up_grad], axis=1))
    grads = jnp.concatenate(grads, axis=0)
    grads = lax.dot_general(pick, grads, NN, preferred_element_type=jnp.float32).astype(jnp.bfloat16)
    for q in range(4):
        pair = w_ref[2 * q : 2 * q + 2].reshape(2 * ROWS, 2 * COLS)
        part = lax.dot_general(grads, pair, NT, preferred_element_type=jnp.float32)
        at = slice(q * 2 * ROWS, (q + 1) * 2 * ROWS)
        out_ref[:, :, at] = part.astype(jnp.bfloat16).reshape(N_X, 48, 2 * ROWS)


def input_send_kernel(pos_ref, *refs):
    input_part(pos_ref, *refs, 1 - pos_ref[1])


def input_keep_kernel(pos_ref, *refs):
    input_part(pos_ref, *refs, pos_ref[1])


def add_kernel(a_ref, b_ref, out_ref):
    out_ref[...] = (a_ref[...].astype(jnp.float32) + b_ref[...].astype(jnp.float32)).astype(jnp.bfloat16)


def x_sum_kernel(parts_ref, out_ref):
    total = parts_ref[0].astype(jnp.float32)
    for i in range(1, N_X):
        total += parts_ref[i].astype(jnp.float32)
    total = total.astype(jnp.bfloat16)
    row = lax.broadcasted_iota(jnp.int32, (N_Y * 24, 48), 0)
    col = lax.broadcasted_iota(jnp.int32, (N_Y * 24, 48), 1)
    k = (row * 2731) >> 16
    left = row - 24 * k
    packed = None
    for q in range(4):
        inside = (left >= 6 * q) & (left < 6 * q + 6)
        pick = jnp.where(inside & (k * 6 + left - 6 * q == col), 1.0, 0.0).astype(jnp.bfloat16)
        part = total[:, q * QUARTER : (q + 1) * QUARTER]
        part = lax.dot_general(pick, part, NN, preferred_element_type=jnp.float32)
        packed = part if packed is None else packed + part
    out_ref[...] = packed.astype(jnp.bfloat16)


def input_sum_kernel(parts_ref, out_ref):
    row = lax.broadcasted_iota(jnp.int32, (8, 24), 0)
    col = lax.broadcasted_iota(jnp.int32, (8, 24), 1)
    for z in range(2):
        total = parts_ref[4 * z].astype(jnp.float32)
        for i in range(1, 4):
            total += parts_ref[4 * z + i].astype(jnp.float32)
        total = total.astype(jnp.bfloat16)
        for q in range(4):
            pick = jnp.where((row + 6 * q == col) & (row < 6), 1.0, 0.0).astype(jnp.bfloat16)
            part = lax.dot_general(pick, total, NN, preferred_element_type=jnp.float32)
            at = z * HALF + q * QUARTER
            out_ref[:, at : at + QUARTER] = part[:6].astype(jnp.bfloat16)


VMEM = pl.BlockSpec(memory_space=pltpu.VMEM)
SMEM = pl.BlockSpec(memory_space=pltpu.SMEM)
HBM = pl.BlockSpec(memory_space=pltpu.HBM)


def call(kernel, out_shapes, *args, name, flops=0, scratch=(), hbm=(), limit=16):
    specs = [SMEM if a.dtype == jnp.int32 and a.ndim == 1 else HBM if i in hbm else VMEM for i, a in enumerate(args)]
    moved = 0
    if flops:
        moved = sum(a.size * a.dtype.itemsize for a in args)
        moved += sum(o.size * o.dtype.itemsize for o in jax.tree.leaves(out_shapes))
    return pl.pallas_call(
        kernel,
        out_shape=out_shapes,
        in_specs=specs,
        out_specs=jax.tree.map(lambda _: VMEM, out_shapes),
        scratch_shapes=scratch,
        compiler_params=pltpu.CompilerParams(vmem_limit_bytes=limit * 2**20),
        cost_estimate=pl.CostEstimate(flops=flops, bytes_accessed=moved, transcendentals=0),
        name=name,
    )(*args)


def shaped(shape, dtype=jnp.bfloat16):
    return jax.ShapeDtypeStruct(shape, dtype)


def on_device(inputs, grad_out, gate_codes, up_codes, down_codes):
    dp, tensor = lax.axis_index("dp"), lax.axis_index("tensor")
    pos = jnp.stack([dp // N_Y, tensor % 2, dp % N_Y, tensor // 2 % N_ZL]).astype(jnp.int32)
    wide, bf16, f32 = 3 * COLS, jnp.bfloat16, jnp.float32

    w, down_w = call(
        decode_kernel, (shaped((2, FEAT, wide)), shaped((ROWS, COLS), f32)), gate_codes, up_codes, down_codes,
        name="decode", flops=ROWS * COLS * 32,
        scratch=[pltpu.VMEM((3, ROWS, COLS), jnp.int32), pltpu.SemaphoreType.DMA((3,))], hbm=(0, 1, 2), limit=60,
    )
    w = lax.all_gather(w, "dp", axis=0, axis_index_groups=Y_GROUPS)

    def folded(acts):
        acts = acts.T
        return jnp.concatenate([acts[:HALF_FEAT], acts[HALF_FEAT:]], axis=1)

    acts = jnp.concatenate([folded(inputs), folded(grad_out)], axis=0)
    acts = jnp.stack([lax.ppermute(acts, ("dp", "tensor"), turn) for turn in TURNS])
    acts = jnp.broadcast_to(acts[None], (N_X, N_ZL, FEAT, 2 * TOK))
    near = lax.all_to_all(acts, "tensor", 0, 0, axis_index_groups=X_GROUPS, tiled=True)
    far = lax.ppermute(near, "tensor", CORE_SWAP)

    flops = HALF * COLS * 2 * TOK
    gate_up_shape, hidden_grad_shape = (2, TOK, 2 * COLS), (2, TOK, COLS)
    gate_up, hidden_grad = call(
        near_kernel, (shaped(gate_up_shape, f32), shaped(hidden_grad_shape, f32)), pos, near, w,
        name="forward_near", flops=3 * flops,
    )
    own, send = call(
        functools.partial(far_kernel, 0), (shaped(gate_up_shape, f32), shaped(gate_up_shape)), pos, far, w, gate_up,
        name="gate_up",
    )
    got = lax.ppermute(send, "dp", Z_SWAP)
    own_hg, send = call(
        functools.partial(far_kernel, 1), (shaped(hidden_grad_shape, f32), shaped(hidden_grad_shape)), pos, far, w,
        hidden_grad, name="hidden_grad",
    )
    got_hg = lax.ppermute(send, "dp", Z_SWAP)
    w_own, _ = lax.optimization_barrier((w, own_hg))
    w_gate_up = call(copy_kernel, shaped((N_Y, 2, FEAT, 2 * COLS)), w_own, name="copy", flops=flops)

    got, own_hg = lax.optimization_barrier((got, own_hg))
    down = call(down_kernel, shaped((N_Y, 2, FEAT, COLS)), pos, near, far, own, got, name="down")
    down_grad = lax.psum_scatter(
        down.reshape(N_Y * ROWS, COLS), "dp", scatter_dimension=0, axis_index_groups=Y_GROUPS, tiled=True
    )
    down, got_hg, w_gate_up = lax.optimization_barrier((down, got_hg, w_gate_up))

    out = shaped((N_X, 48, HALF))
    grads = (own, got, own_hg, got_hg)
    send = call(input_send_kernel, out, pos, *grads, w_gate_up, name="input_send", flops=flops)
    other = lax.ppermute(send, "tensor", CORE_SWAP)
    keep = call(input_keep_kernel, out, pos, *grads, w_gate_up, name="input_keep", flops=flops)
    parts = call(add_kernel, out, keep, other, name="add")
    parts = lax.all_to_all(parts, "tensor", 0, 0, axis_index_groups=X_GROUPS, tiled=True)
    parts = call(x_sum_kernel, shaped((N_Y * 24, QUARTER)), parts, name="x_sum", flops=35 * 10**8).reshape(N_Y, 24, QUARTER)
    parts = lax.all_to_all(parts, ("dp", "tensor"), 0, 0, axis_index_groups=Z_GROUPS, tiled=True)
    input_grad = call(input_sum_kernel, shaped((6, D)), parts, name="input_sum")
    down_log_grad = down_grad.astype(f32) * down_w
    return input_grad, down_log_grad


def solution(mesh):
    in_specs = (P("dp", "tensor"),) * 5
    out_specs = (P(("dp", "tensor"), None), P("dp", "tensor"))
    return jax.shard_map(on_device, mesh=mesh, in_specs=in_specs, out_specs=out_specs, check_vma=False)
```

```python
import math

import jax
import jax.numpy as jnp
from jax import lax
from jax.experimental import pallas as pl
from jax.experimental.pallas import tpu as pltpu
from jax.sharding import PartitionSpec as P

D = 5120
FF_W = 8192
N_Z, N_Y, N_X, N_ZL = 2, 8, 4, 4
N_T = N_X * N_ZL * 2
TOK = 192
FEAT = 160
HALF_FEAT = 80
ROWS = 320
COLS = 256
HALF = D // 2
QUARTER = HALF // 4

coef_one = 0.6931472
coef_two = 0.2402265
coef_three = 0.0555041

NN = (((1,), (0,)), ((), ()))
NT = (((1,), (1,)), ((), ()))


def _turn_pairs(step):
    pairs = []
    for z in range(N_Z):
        for y in range(N_Y):
            for t in range(N_T):
                x1, rest = t // 16, (t % 16) ^ (2 * step)
                pairs.append(((z * N_Y + y) * N_T + t, (x1 * N_Y + y) * N_T + (1 - z) * 16 + rest))
    return pairs


TURNS = [_turn_pairs(step) for step in range(N_ZL)]
Z_SWAP = [(d, (d + N_Y) % (N_Z * N_Y)) for d in range(N_Z * N_Y)]
CORE_SWAP = [(t, t ^ 1) for t in range(N_T)]
ZL_GROUPS = [[x * 8 + zl * 2 + c for zl in range(N_ZL)] for x in range(N_X) for c in range(2)]
X_GROUPS = [[x * 8 + i for x in range(N_X)] for i in range(8)]
Y_GROUPS = [[z * N_Y + y for y in range(N_Y)] for z in range(N_Z)]
Z_GROUPS = [
    [(z * N_Y + y) * N_T + x * 8 + zl * 2 + c for z in range(N_Z) for zl in range(N_ZL)]
    for y in range(N_Y)
    for x in range(N_X)
    for c in range(2)
]


def decode(packed, fan):
    frac = ((packed >> 1) & 7).astype(jnp.float32) * 0.125
    power = jnp.where((packed & 16) != 0, 0.5, 1.0)
    power = power * jnp.where((packed & 32) != 0, 0.25, 1.0)
    power = power * jnp.where((packed & 64) != 0, 0.0625, 1.0)
    poly = 1.0 - frac * (coef_one - frac * (coef_two - coef_three * frac))
    value = power * poly * (3.0 / math.sqrt(fan))
    return jnp.where((packed & 1) != 0, -value, value)


def decode_kernel(gate_ref, up_ref, down_ref, out_ref, codes, values, in_sems, out_sems):
    pieces = [(i, core) for i in range(3) for core in range(2)]
    reads, writes = [], []
    for n, (i, core) in enumerate(pieces):
        ref = (gate_ref, up_ref, down_ref)[i].at[core * FEAT : (core + 1) * FEAT]
        reads.append(pltpu.make_async_copy(ref, codes.at[n], in_sems.at[n]))
        writes.append(
            pltpu.make_async_copy(values.at[n], out_ref.at[core, :, i * COLS : (i + 1) * COLS], out_sems.at[n])
        )
        reads[n].start()
    for n, (i, core) in enumerate(pieces):
        reads[n].wait()
        values[n] = decode(codes[n], (D, D, FF_W)[i]).astype(jnp.bfloat16)
        writes[n].start()
    for write in writes:
        write.wait()


def decode_down_kernel(codes_ref, out_ref):
    out_ref[...] = decode(codes_ref[...], FF_W)


def fetch(w_ref, which, cols, w, sems):
    copies = [pltpu.make_async_copy(w_ref.at[y, which, :, cols], w.at[y], sems.at[y]) for y in range(N_Y)]
    for copy in copies:
        copy.start()
    return copies


def fetch_acts(acts_ref, kind, acts, sems):
    rows = slice(kind * HALF_FEAT, (kind + 1) * HALF_FEAT)
    copies = [pltpu.make_async_copy(acts_ref.at[x, :, rows], acts.at[x], sems.at[x]) for x in range(N_X)]
    for copy in copies:
        copy.start()
    return copies


def block(acts_ref, x, my_zl, row):
    return jnp.concatenate([acts_ref[x, zl ^ my_zl, row : row + HALF_FEAT] for zl in range(N_ZL)], axis=0)


def forward(acts_ref, my_zl, row, w, ready):
    sums = [None, None]
    for x0 in range(2):
        ready(x0)
        acts = [block(acts_ref, 2 - 2 * h + x0, my_zl, row).T for h in range(2)]
        for half in range(2):
            rows = slice(half * HALF_FEAT, (half + 1) * HALF_FEAT)
            weights = jnp.concatenate([w(x0 * N_ZL + zl, rows) for zl in range(N_ZL)], axis=0)
            for h in range(2):
                part = acts[h][half * TOK : (half + 1) * TOK]
                part = lax.dot_general(part, weights, NN, preferred_element_type=jnp.float32)
                sums[h] = part if sums[h] is None else sums[h] + part
    return sums


GATE_UP, HIDDEN_GRAD = slice(0, 2 * COLS), slice(2 * COLS, 3 * COLS)


def near_kernel(pos_ref, acts_ref, w_ref, out_ref, w_far_ref, w, sems):
    core = pos_ref[1]
    copies = fetch(w_ref, core, GATE_UP, w, sems.at[0])
    others = fetch(w_ref, 1 - core, GATE_UP, w_far_ref, sems.at[1])

    def ready(x0):
        for copy in copies[x0 * N_ZL : (x0 + 1) * N_ZL]:
            copy.wait()

    for h, total in enumerate(forward(acts_ref, pos_ref[3], 0, lambda y, rows: w[y, rows], ready)):
        out_ref[h] = total
    for copy in others:
        copy.wait()


def gate_up_kernel(pos_ref, acts_ref, near_ref, w_far_ref, own_ref, send_ref, acts, sems):
    copies = fetch_acts(acts_ref, 0, acts, sems)

    def ready(x0):
        copies[x0].wait()
        copies[2 + x0].wait()

    for h, total in enumerate(forward(acts, pos_ref[3], 0, lambda y, rows: w_far_ref[y, rows], ready)):
        total += near_ref[h]
        own_ref[h] = total
        send_ref[h] = total.astype(jnp.bfloat16)


def hidden_grad_kernel(pos_ref, near_ref, far_ref, w_ref, own_ref, send_ref, grads_ref, acts, sems):
    core, my_zl = pos_ref[1], pos_ref[3]
    copies = fetch_acts(far_ref, 1, acts, sems)
    totals = forward(near_ref, my_zl, HALF_FEAT, lambda y, rows: w_ref[y, core, rows, HIDDEN_GRAD], lambda x0: None)
    for copy in copies:
        copy.wait()
    far = forward(acts, my_zl, 0, lambda y, rows: w_ref[y, 1 - core, rows, HIDDEN_GRAD], lambda x0: None)
    for h in range(2):
        total = totals[h] + far[h]
        own_ref[h] = total
        send_ref[h] = total.astype(jnp.bfloat16)
    for side, (ref, row) in enumerate(((near_ref, HALF_FEAT), (acts, 0))):
        for x0 in range(2):
            for h in range(2):
                grads_ref[side, x0, :, h * 2 * TOK : (h + 1) * 2 * TOK] = block(ref, 2 - 2 * h + x0, my_zl, row)


def copy_kernel(w_ref, out_ref):
    out_ref[...] = w_ref[:, :, :, : 2 * COLS]


def down_kernel(pos_ref, grads_ref, own_ref, got_ref, out_ref):
    core = pos_ref[1]
    blank = jnp.zeros((TOK, COLS), jnp.bfloat16)
    rows = []
    for h in range(2):
        total = own_ref[h] + got_ref[h].astype(jnp.float32)
        gate, up = total[:, :COLS], total[:, COLS:]
        hidden = (gate * jax.nn.sigmoid(gate) * up).astype(jnp.bfloat16)
        rows += [jnp.concatenate([hidden, blank], axis=1), jnp.concatenate([blank, hidden], axis=1)]
    hidden = jnp.concatenate(rows, axis=0)
    for x0 in range(2):
        for side, which in ((0, core), (1, 1 - core)):
            acts = grads_ref[side, x0]
            part = lax.dot_general(acts, hidden, NN, preferred_element_type=jnp.float32).astype(jnp.bfloat16)
            for zl in range(N_ZL):
                rows = part[zl * HALF_FEAT : (zl + 1) * HALF_FEAT]
                out_ref[x0 * N_ZL + zl, which, :HALF_FEAT] = rows[:, :COLS]
                out_ref[x0 * N_ZL + zl, which, HALF_FEAT:] = rows[:, COLS:]


def input_part(pos_ref, own_ref, got_ref, own_hg_ref, got_hg_ref, w_ref, out_ref, side):
    rows = N_X * 48
    row = lax.broadcasted_iota(jnp.int32, (rows, 2 * TOK), 0)
    col = lax.broadcasted_iota(jnp.int32, (rows, 2 * TOK), 1)
    x = (row * 1366) >> 16
    left = row - 48 * x
    h = jnp.where(left >= 24, 1, 0)
    left = left - 24 * h
    zl = (left * 10923) >> 16
    wanted = h * TOK + x * 48 + zl * 12 + side * 6 + left - 6 * zl
    pick = jnp.where(wanted == col, 1.0, 0.0).astype(jnp.bfloat16)
    grads = []
    for h in range(2):
        total = own_ref[h] + got_ref[h].astype(jnp.float32)
        gate, up = total[:, :COLS], total[:, COLS:]
        hidden_grad = own_hg_ref[h] + got_hg_ref[h].astype(jnp.float32)
        sig = jax.nn.sigmoid(gate)
        gate_grad = (hidden_grad * up * sig * (1.0 + gate * (1.0 - sig))).astype(jnp.bfloat16)
        up_grad = (hidden_grad * gate * sig).astype(jnp.bfloat16)
        grads.append(jnp.concatenate([gate_grad, up_grad], axis=1))
    grads = jnp.concatenate(grads, axis=0)
    grads = lax.dot_general(pick, grads, NN, preferred_element_type=jnp.float32).astype(jnp.bfloat16)
    for q in range(4):
        pair = w_ref[2 * q : 2 * q + 2].reshape(2 * ROWS, 2 * COLS)
        part = lax.dot_general(grads, pair, NT, preferred_element_type=jnp.float32)
        at = slice(q * 2 * ROWS, (q + 1) * 2 * ROWS)
        out_ref[:, :, at] = part.astype(jnp.bfloat16).reshape(N_X, 48, 2 * ROWS)


def input_send_kernel(pos_ref, *refs):
    input_part(pos_ref, *refs, 1 - pos_ref[1])


def input_keep_kernel(pos_ref, *refs):
    input_part(pos_ref, *refs, pos_ref[1])


def add_kernel(a_ref, b_ref, out_ref):
    out_ref[...] = (a_ref[...].astype(jnp.float32) + b_ref[...].astype(jnp.float32)).astype(jnp.bfloat16)


def x_sum_kernel(parts_ref, out_ref):
    total = parts_ref[0].astype(jnp.float32)
    for i in range(1, N_X):
        total += parts_ref[i].astype(jnp.float32)
    total = total.astype(jnp.bfloat16)
    row = lax.broadcasted_iota(jnp.int32, (N_Y * 24, 48), 0)
    col = lax.broadcasted_iota(jnp.int32, (N_Y * 24, 48), 1)
    k = (row * 2731) >> 16
    left = row - 24 * k
    packed = None
    for q in range(4):
        inside = (left >= 6 * q) & (left < 6 * q + 6)
        pick = jnp.where(inside & (k * 6 + left - 6 * q == col), 1.0, 0.0).astype(jnp.bfloat16)
        part = total[:, q * QUARTER : (q + 1) * QUARTER]
        part = lax.dot_general(pick, part, NN, preferred_element_type=jnp.float32)
        packed = part if packed is None else packed + part
    out_ref[...] = packed.astype(jnp.bfloat16)


def input_sum_kernel(parts_ref, out_ref):
    row = lax.broadcasted_iota(jnp.int32, (8, 24), 0)
    col = lax.broadcasted_iota(jnp.int32, (8, 24), 1)
    for z in range(2):
        total = parts_ref[4 * z].astype(jnp.float32)
        for i in range(1, 4):
            total += parts_ref[4 * z + i].astype(jnp.float32)
        total = total.astype(jnp.bfloat16)
        for q in range(4):
            pick = jnp.where((row + 6 * q == col) & (row < 6), 1.0, 0.0).astype(jnp.bfloat16)
            part = lax.dot_general(pick, total, NN, preferred_element_type=jnp.float32)
            at = z * HALF + q * QUARTER
            out_ref[:, at : at + QUARTER] = part[:6].astype(jnp.bfloat16)


VMEM = pl.BlockSpec(memory_space=pltpu.VMEM)
SMEM = pl.BlockSpec(memory_space=pltpu.SMEM)
HBM = pl.BlockSpec(memory_space=pltpu.HBM)


def call(kernel, out_shapes, *args, name, flops=0, scratch=(), hbm=(), limit=16, out_spec=VMEM):
    specs = [SMEM if a.dtype == jnp.int32 and a.ndim == 1 else HBM if i in hbm else VMEM for i, a in enumerate(args)]
    moved = 0
    if flops:
        moved = sum(a.size * a.dtype.itemsize for a in args)
        moved += sum(o.size * o.dtype.itemsize for o in jax.tree.leaves(out_shapes))
    return pl.pallas_call(
        kernel,
        out_shape=out_shapes,
        in_specs=specs,
        out_specs=jax.tree.map(lambda _: out_spec, out_shapes),
        scratch_shapes=scratch,
        compiler_params=pltpu.CompilerParams(vmem_limit_bytes=limit * 2**20),
        cost_estimate=pl.CostEstimate(flops=flops, bytes_accessed=moved, transcendentals=0),
        name=name,
    )(*args)


def shaped(shape, dtype=jnp.bfloat16):
    return jax.ShapeDtypeStruct(shape, dtype)


def on_device(inputs, grad_out, gate_codes, up_codes, down_codes):
    dp, tensor = lax.axis_index("dp"), lax.axis_index("tensor")
    pos = jnp.stack([dp // N_Y, tensor % 2, dp % N_Y, tensor // 2 % N_ZL]).astype(jnp.int32)
    wide, bf16, f32 = 3 * COLS, jnp.bfloat16, jnp.float32

    w = call(
        decode_kernel, shaped((2, FEAT, wide)), gate_codes, up_codes, down_codes,
        name="decode", flops=ROWS * COLS * 32,
        scratch=[
            pltpu.VMEM((6, FEAT, COLS), jnp.int32), pltpu.VMEM((6, FEAT, COLS), bf16),
            pltpu.SemaphoreType.DMA((6,)), pltpu.SemaphoreType.DMA((6,)),
        ],
        hbm=(0, 1, 2), limit=60, out_spec=HBM,
    )
    w = lax.all_gather(w, "dp", axis=0, axis_index_groups=Y_GROUPS)

    def folded(acts):
        acts = acts.T
        return jnp.concatenate([acts[:HALF_FEAT], acts[HALF_FEAT:]], axis=1)

    acts = jnp.concatenate([folded(inputs), folded(grad_out)], axis=0)
    acts = jnp.stack([lax.ppermute(acts, ("dp", "tensor"), turn) for turn in TURNS])
    acts = jnp.broadcast_to(acts[None], (N_X, N_ZL, FEAT, 2 * TOK))
    near = lax.all_to_all(acts, "tensor", 0, 0, axis_index_groups=X_GROUPS, tiled=True)
    far = lax.ppermute(near, "tensor", CORE_SWAP)

    flops = HALF * COLS * 2 * TOK
    gate_up_shape, hidden_grad_shape = (2, TOK, 2 * COLS), (2, TOK, COLS)
    w_shape = (N_Y, FEAT, 2 * COLS)
    acts_space = [pltpu.VMEM((N_X, N_ZL, HALF_FEAT, 2 * TOK), bf16), pltpu.SemaphoreType.DMA((N_X,))]
    gate_up, w_far = call(
        near_kernel, (shaped(gate_up_shape, f32), shaped(w_shape)), pos, near, w, name="forward_near", flops=2 * flops,
        hbm=(2,), limit=50, scratch=[pltpu.VMEM(w_shape, bf16), pltpu.SemaphoreType.DMA((2, N_Y))],
    )
    own, send = call(
        gate_up_kernel, (shaped(gate_up_shape, f32), shaped(gate_up_shape)), pos, far, gate_up, w_far, name="gate_up",
        hbm=(1,), scratch=acts_space,
    )
    got = lax.ppermute(send, "dp", Z_SWAP)
    own_hg, send, grads = call(
        hidden_grad_kernel,
        (shaped(hidden_grad_shape, f32), shaped(hidden_grad_shape), shaped((2, 2, N_ZL * HALF_FEAT, 4 * TOK))),
        pos, near, far, w, name="hidden_grad", hbm=(2,), scratch=acts_space,
    )
    got_hg = lax.ppermute(send, "dp", Z_SWAP)
    w_own, codes, _ = lax.optimization_barrier((w, down_codes, own_hg))
    down_w = call(decode_down_kernel, shaped((ROWS, COLS), f32), codes, name="decode_down", flops=ROWS * COLS * 32)
    w_gate_up = call(copy_kernel, shaped((N_Y, 2, FEAT, 2 * COLS)), w_own, name="copy", flops=flops)

    got, own_hg = lax.optimization_barrier((got, own_hg))
    down = call(down_kernel, shaped((N_Y, 2, FEAT, COLS)), pos, grads, own, got, name="down")
    down_grad = lax.psum_scatter(
        down.reshape(N_Y * ROWS, COLS), "dp", scatter_dimension=0, axis_index_groups=Y_GROUPS, tiled=True
    )
    down, got_hg, w_gate_up, down_w = lax.optimization_barrier((down, got_hg, w_gate_up, down_w))

    out = shaped((N_X, 48, HALF))
    grads = (own, got, own_hg, got_hg)
    send = call(input_send_kernel, out, pos, *grads, w_gate_up, name="input_send", flops=flops)
    other = lax.ppermute(send, "tensor", CORE_SWAP)
    keep = call(input_keep_kernel, out, pos, *grads, w_gate_up, name="input_keep", flops=flops)
    parts = call(add_kernel, out, keep, other, name="add")
    parts = lax.all_to_all(parts, "tensor", 0, 0, axis_index_groups=X_GROUPS, tiled=True)
    parts = call(x_sum_kernel, shaped((N_Y * 24, QUARTER)), parts, name="x_sum", flops=35 * 10**8).reshape(N_Y, 24, QUARTER)
    parts = lax.all_to_all(parts, ("dp", "tensor"), 0, 0, axis_index_groups=Z_GROUPS, tiled=True)
    input_grad = call(input_sum_kernel, shaped((6, D)), parts, name="input_sum")
    down_log_grad = down_grad.astype(f32) * down_w
    return input_grad, down_log_grad


def solution(mesh):
    in_specs = (P("dp", "tensor"),) * 5
    out_specs = (P(("dp", "tensor"), None), P("dp", "tensor"))
    return jax.shard_map(on_device, mesh=mesh, in_specs=in_specs, out_specs=out_specs, check_vma=False)
```

```python
import math

import jax
import jax.numpy as jnp
from jax import lax
from jax.experimental import pallas as pl
from jax.experimental.pallas import tpu as pltpu
from jax.sharding import PartitionSpec as P

D = 5120
FF_W = 8192
N_Z, N_Y, N_X, N_ZL = 2, 8, 4, 4
N_T = N_X * N_ZL * 2
TOK = 192
FEAT = 160
HALF_FEAT = 80
ROWS = 320
COLS = 256
HALF = D // 2
QUARTER = HALF // 4

coef_one = 0.6931472
coef_two = 0.2402265
coef_three = 0.0555041

NN = (((1,), (0,)), ((), ()))
NT = (((1,), (1,)), ((), ()))


def _turn_pairs(step):
    pairs = []
    for z in range(N_Z):
        for y in range(N_Y):
            for t in range(N_T):
                x1, rest = t // 16, (t % 16) ^ (2 * step)
                pairs.append(((z * N_Y + y) * N_T + t, (x1 * N_Y + y) * N_T + (1 - z) * 16 + rest))
    return pairs


TURNS = [_turn_pairs(step) for step in range(N_ZL)]
Z_SWAP = [(d, (d + N_Y) % (N_Z * N_Y)) for d in range(N_Z * N_Y)]
CORE_SWAP = [(t, t ^ 1) for t in range(N_T)]
ZL_GROUPS = [[x * 8 + zl * 2 + c for zl in range(N_ZL)] for x in range(N_X) for c in range(2)]
X_GROUPS = [[x * 8 + i for x in range(N_X)] for i in range(8)]
Y_GROUPS = [[z * N_Y + y for y in range(N_Y)] for z in range(N_Z)]
Z_GROUPS = [
    [(z * N_Y + y) * N_T + x * 8 + zl * 2 + c for z in range(N_Z) for zl in range(N_ZL)]
    for y in range(N_Y)
    for x in range(N_X)
    for c in range(2)
]


def decode(packed, fan):
    frac = (packed & 14).astype(jnp.float32)
    poly = 1.0 - frac * (coef_one / 16 - frac * (coef_two / 256 - coef_three / 4096 * frac))
    power = lax.shift_right_logical(jnp.full_like(packed, 128), packed >> 4)
    power = jnp.where((packed & 1) != 0, -power, power).astype(jnp.float32)
    return power * (3.0 / math.sqrt(fan) / 128) * poly


def decode_kernel(gate_ref, up_ref, down_ref, out_ref, codes, values, in_sems, out_sems):
    pieces = [(i, core) for i in range(3) for core in range(2)]
    reads, writes = [], []
    for n, (i, core) in enumerate(pieces):
        ref = (gate_ref, up_ref, down_ref)[i].at[core * FEAT : (core + 1) * FEAT]
        reads.append(pltpu.make_async_copy(ref, codes.at[n], in_sems.at[n]))
        writes.append(
            pltpu.make_async_copy(values.at[n], out_ref.at[core, :, i * COLS : (i + 1) * COLS], out_sems.at[n])
        )
        reads[n].start()
    for n, (i, core) in enumerate(pieces):
        reads[n].wait()
        values[n] = decode(codes[n], (D, D, FF_W)[i]).astype(jnp.bfloat16)
        writes[n].start()
    for write in writes:
        write.wait()


def decode_down_kernel(codes_ref, out_ref):
    out_ref[...] = decode(codes_ref[...], FF_W)


def fetch(w_ref, which, cols, w, sems):
    copies = [pltpu.make_async_copy(w_ref.at[y, which, :, cols], w.at[y], sems.at[y]) for y in range(N_Y)]
    for copy in copies:
        copy.start()
    return copies


def fetch_acts(acts_ref, kind, acts, sems):
    rows = slice(kind * HALF_FEAT, (kind + 1) * HALF_FEAT)
    copies = [pltpu.make_async_copy(acts_ref.at[x, :, rows], acts.at[x], sems.at[x]) for x in range(N_X)]
    for copy in copies:
        copy.start()
    return copies


def block(acts_ref, x, my_zl, row):
    return jnp.concatenate([acts_ref[x, zl ^ my_zl, row : row + HALF_FEAT] for zl in range(N_ZL)], axis=0)


def forward(acts_ref, my_zl, row, w, acts_ready=None, w_ready=None):
    sums = [None, None]
    for x0 in range(2):
        if acts_ready is not None:
            acts_ready(x0)
        acts = [block(acts_ref, 2 - 2 * h + x0, my_zl, row).T for h in range(2)]
        if w_ready is not None:
            w_ready(x0)
        for half in range(2):
            rows = slice(half * HALF_FEAT, (half + 1) * HALF_FEAT)
            weights = jnp.concatenate([w(x0 * N_ZL + zl, rows) for zl in range(N_ZL)], axis=0)
            for h in range(2):
                part = acts[h][half * TOK : (half + 1) * TOK]
                part = lax.dot_general(part, weights, NN, preferred_element_type=jnp.float32)
                sums[h] = part if sums[h] is None else sums[h] + part
    return sums


GATE_UP, HIDDEN_GRAD = slice(0, 2 * COLS), slice(2 * COLS, 3 * COLS)


def near_kernel(pos_ref, acts_ref, w_ref, out_ref, w_far_ref, w, sems):
    core = pos_ref[1]
    copies = fetch(w_ref, core, GATE_UP, w, sems.at[0])
    others = fetch(w_ref, 1 - core, GATE_UP, w_far_ref, sems.at[1])

    def ready(x0):
        for copy in copies[x0 * N_ZL : (x0 + 1) * N_ZL]:
            copy.wait()

    for h, total in enumerate(forward(acts_ref, pos_ref[3], 0, lambda y, rows: w[y, rows], w_ready=ready)):
        out_ref[h] = total
    for copy in others:
        copy.wait()


def gate_up_kernel(pos_ref, acts_ref, near_ref, w_far_ref, own_ref, send_ref, acts, sems):
    copies = fetch_acts(acts_ref, 0, acts, sems)

    def ready(x0):
        copies[x0].wait()
        copies[2 + x0].wait()

    for h, total in enumerate(forward(acts, pos_ref[3], 0, lambda y, rows: w_far_ref[y, rows], acts_ready=ready)):
        total += near_ref[h]
        own_ref[h] = total
        send_ref[h] = total.astype(jnp.bfloat16)


def hidden_grad_kernel(pos_ref, near_ref, far_ref, w_ref, own_ref, send_ref, grads_ref, acts, sems):
    core, my_zl = pos_ref[1], pos_ref[3]
    copies = fetch_acts(far_ref, 1, acts, sems)
    totals = forward(near_ref, my_zl, HALF_FEAT, lambda y, rows: w_ref[y, core, rows, HIDDEN_GRAD])
    for copy in copies:
        copy.wait()
    far = forward(acts, my_zl, 0, lambda y, rows: w_ref[y, 1 - core, rows, HIDDEN_GRAD])
    for h in range(2):
        total = totals[h] + far[h]
        own_ref[h] = total
        send_ref[h] = total.astype(jnp.bfloat16)
    for side, (ref, row) in enumerate(((near_ref, HALF_FEAT), (acts, 0))):
        for x0 in range(2):
            for h in range(2):
                grads_ref[side, x0, :, h * 2 * TOK : (h + 1) * 2 * TOK] = block(ref, 2 - 2 * h + x0, my_zl, row)


def copy_kernel(w_ref, out_ref):
    out_ref[...] = w_ref[:, :, :, : 2 * COLS]


def down_kernel(pos_ref, grads_ref, own_ref, got_ref, out_ref):
    core = pos_ref[1]
    blank = jnp.zeros((TOK, COLS), jnp.bfloat16)
    rows = []
    for h in range(2):
        total = own_ref[h] + got_ref[h].astype(jnp.float32)
        gate, up = total[:, :COLS], total[:, COLS:]
        hidden = (gate * jax.nn.sigmoid(gate) * up).astype(jnp.bfloat16)
        rows += [jnp.concatenate([hidden, blank], axis=1), jnp.concatenate([blank, hidden], axis=1)]
    hidden = jnp.concatenate(rows, axis=0)
    for x0 in range(2):
        for side, which in ((0, core), (1, 1 - core)):
            acts = grads_ref[side, x0]
            part = lax.dot_general(acts, hidden, NN, preferred_element_type=jnp.float32).astype(jnp.bfloat16)
            for zl in range(N_ZL):
                rows = part[zl * HALF_FEAT : (zl + 1) * HALF_FEAT]
                out_ref[x0 * N_ZL + zl, which, :HALF_FEAT] = rows[:, :COLS]
                out_ref[x0 * N_ZL + zl, which, HALF_FEAT:] = rows[:, COLS:]


def input_part(grads, w_ref, out_ref, side):
    rows = N_X * 48
    row = lax.broadcasted_iota(jnp.int32, (rows, 2 * TOK), 0)
    col = lax.broadcasted_iota(jnp.int32, (rows, 2 * TOK), 1)
    x = (row * 1366) >> 16
    left = row - 48 * x
    h = jnp.where(left >= 24, 1, 0)
    left = left - 24 * h
    zl = (left * 10923) >> 16
    wanted = h * TOK + x * 48 + zl * 12 + side * 6 + left - 6 * zl
    pick = jnp.where(wanted == col, 1.0, 0.0).astype(jnp.bfloat16)
    grads = lax.dot_general(pick, grads, NN, preferred_element_type=jnp.float32).astype(jnp.bfloat16)
    for q in range(4):
        pair = w_ref[2 * q : 2 * q + 2].reshape(2 * ROWS, 2 * COLS)
        part = lax.dot_general(grads, pair, NT, preferred_element_type=jnp.float32)
        at = slice(q * 2 * ROWS, (q + 1) * 2 * ROWS)
        out_ref[:, :, at] = part.astype(jnp.bfloat16).reshape(N_X, 48, 2 * ROWS)


def input_send_kernel(pos_ref, own_ref, got_ref, own_hg_ref, got_hg_ref, w_ref, out_ref, grads_ref):
    grads = []
    for h in range(2):
        total = own_ref[h] + got_ref[h].astype(jnp.float32)
        gate, up = total[:, :COLS], total[:, COLS:]
        hidden_grad = own_hg_ref[h] + got_hg_ref[h].astype(jnp.float32)
        sig = jax.nn.sigmoid(gate)
        gate_grad = (hidden_grad * up * sig * (1.0 + gate * (1.0 - sig))).astype(jnp.bfloat16)
        up_grad = (hidden_grad * gate * sig).astype(jnp.bfloat16)
        grads.append(jnp.concatenate([gate_grad, up_grad], axis=1))
    grads = jnp.concatenate(grads, axis=0)
    grads_ref[...] = grads
    input_part(grads, w_ref, out_ref, 1 - pos_ref[1])


def input_keep_kernel(pos_ref, grads_ref, w_ref, out_ref):
    input_part(grads_ref[...], w_ref, out_ref, pos_ref[1])


def add_kernel(a_ref, b_ref, out_ref):
    out_ref[...] = (a_ref[...].astype(jnp.float32) + b_ref[...].astype(jnp.float32)).astype(jnp.bfloat16)


def x_sum_kernel(parts_ref, out_ref):
    total = parts_ref[0].astype(jnp.float32)
    for i in range(1, N_X):
        total += parts_ref[i].astype(jnp.float32)
    total = total.astype(jnp.bfloat16)
    row = lax.broadcasted_iota(jnp.int32, (N_Y * 24, 48), 0)
    col = lax.broadcasted_iota(jnp.int32, (N_Y * 24, 48), 1)
    k = (row * 2731) >> 16
    left = row - 24 * k
    packed = None
    for q in range(4):
        inside = (left >= 6 * q) & (left < 6 * q + 6)
        pick = jnp.where(inside & (k * 6 + left - 6 * q == col), 1.0, 0.0).astype(jnp.bfloat16)
        part = total[:, q * QUARTER : (q + 1) * QUARTER]
        part = lax.dot_general(pick, part, NN, preferred_element_type=jnp.float32)
        packed = part if packed is None else packed + part
    out_ref[...] = packed.astype(jnp.bfloat16)


def input_sum_kernel(parts_ref, out_ref):
    row = lax.broadcasted_iota(jnp.int32, (8, 24), 0)
    col = lax.broadcasted_iota(jnp.int32, (8, 24), 1)
    for z in range(2):
        total = parts_ref[4 * z].astype(jnp.float32)
        for i in range(1, 4):
            total += parts_ref[4 * z + i].astype(jnp.float32)
        total = total.astype(jnp.bfloat16)
        for q in range(4):
            pick = jnp.where((row + 6 * q == col) & (row < 6), 1.0, 0.0).astype(jnp.bfloat16)
            part = lax.dot_general(pick, total, NN, preferred_element_type=jnp.float32)
            at = z * HALF + q * QUARTER
            out_ref[:, at : at + QUARTER] = part[:6].astype(jnp.bfloat16)


VMEM = pl.BlockSpec(memory_space=pltpu.VMEM)
SMEM = pl.BlockSpec(memory_space=pltpu.SMEM)
HBM = pl.BlockSpec(memory_space=pltpu.HBM)


def call(kernel, out_shapes, *args, name, flops=0, scratch=(), hbm=(), limit=16, out_spec=VMEM):
    specs = [SMEM if a.dtype == jnp.int32 and a.ndim == 1 else HBM if i in hbm else VMEM for i, a in enumerate(args)]
    moved = 0
    if flops:
        moved = sum(a.size * a.dtype.itemsize for a in args)
        moved += sum(o.size * o.dtype.itemsize for o in jax.tree.leaves(out_shapes))
    return pl.pallas_call(
        kernel,
        out_shape=out_shapes,
        in_specs=specs,
        out_specs=jax.tree.map(lambda _: out_spec, out_shapes),
        scratch_shapes=scratch,
        compiler_params=pltpu.CompilerParams(vmem_limit_bytes=limit * 2**20),
        cost_estimate=pl.CostEstimate(flops=flops, bytes_accessed=moved, transcendentals=0),
        name=name,
    )(*args)


def shaped(shape, dtype=jnp.bfloat16):
    return jax.ShapeDtypeStruct(shape, dtype)


def on_device(inputs, grad_out, gate_codes, up_codes, down_codes):
    dp, tensor = lax.axis_index("dp"), lax.axis_index("tensor")
    pos = jnp.stack([dp // N_Y, tensor % 2, dp % N_Y, tensor // 2 % N_ZL]).astype(jnp.int32)
    wide, bf16, f32 = 3 * COLS, jnp.bfloat16, jnp.float32

    w = call(
        decode_kernel, shaped((2, FEAT, wide)), gate_codes, up_codes, down_codes,
        name="decode", flops=ROWS * COLS * 32,
        scratch=[
            pltpu.VMEM((6, FEAT, COLS), jnp.int32), pltpu.VMEM((6, FEAT, COLS), bf16),
            pltpu.SemaphoreType.DMA((6,)), pltpu.SemaphoreType.DMA((6,)),
        ],
        hbm=(0, 1, 2), limit=60, out_spec=HBM,
    )
    w = lax.all_gather(w, "dp", axis=0, axis_index_groups=Y_GROUPS)

    def folded(acts):
        acts = acts.T
        return jnp.concatenate([acts[:HALF_FEAT], acts[HALF_FEAT:]], axis=1)

    acts = jnp.concatenate([folded(inputs), folded(grad_out)], axis=0)
    acts = jnp.stack([lax.ppermute(acts, ("dp", "tensor"), turn) for turn in TURNS])
    acts = jnp.broadcast_to(acts[None], (N_X, N_ZL, FEAT, 2 * TOK))
    near = lax.all_to_all(acts, "tensor", 0, 0, axis_index_groups=X_GROUPS, tiled=True)
    far = lax.ppermute(near, "tensor", CORE_SWAP)

    flops = HALF * COLS * 2 * TOK
    gate_up_shape, hidden_grad_shape = (2, TOK, 2 * COLS), (2, TOK, COLS)
    w_shape = (N_Y, FEAT, 2 * COLS)
    acts_space = [pltpu.VMEM((N_X, N_ZL, HALF_FEAT, 2 * TOK), bf16), pltpu.SemaphoreType.DMA((N_X,))]
    gate_up, w_far = call(
        near_kernel, (shaped(gate_up_shape, f32), shaped(w_shape)), pos, near, w, name="forward_near", flops=2 * flops,
        hbm=(2,), limit=50, scratch=[pltpu.VMEM(w_shape, bf16), pltpu.SemaphoreType.DMA((2, N_Y))],
    )
    own, send = call(
        gate_up_kernel, (shaped(gate_up_shape, f32), shaped(gate_up_shape)), pos, far, gate_up, w_far, name="gate_up",
        hbm=(1,), scratch=acts_space,
    )
    got = lax.ppermute(send, "dp", Z_SWAP)
    own_hg, send, grads = call(
        hidden_grad_kernel,
        (shaped(hidden_grad_shape, f32), shaped(hidden_grad_shape), shaped((2, 2, N_ZL * HALF_FEAT, 4 * TOK))),
        pos, near, far, w, name="hidden_grad", hbm=(2,), scratch=acts_space,
    )
    got_hg = lax.ppermute(send, "dp", Z_SWAP)
    w_own, codes, _ = lax.optimization_barrier((w, down_codes, own_hg))
    down_w = call(decode_down_kernel, shaped((ROWS, COLS), f32), codes, name="decode_down", flops=ROWS * COLS * 32)
    w_gate_up = call(copy_kernel, shaped((N_Y, 2, FEAT, 2 * COLS)), w_own, name="copy", flops=flops)

    got, own_hg = lax.optimization_barrier((got, own_hg))
    down = call(down_kernel, shaped((N_Y, 2, FEAT, COLS)), pos, grads, own, got, name="down")
    down_grad = lax.psum_scatter(
        down.reshape(N_Y * ROWS, COLS), "dp", scatter_dimension=0, axis_index_groups=Y_GROUPS, tiled=True
    )
    down, got_hg, w_gate_up, down_w = lax.optimization_barrier((down, got_hg, w_gate_up, down_w))

    out = shaped((N_X, 48, HALF))
    send, grads = call(
        input_send_kernel, (out, shaped((2 * TOK, 2 * COLS))), pos, own, got, own_hg, got_hg, w_gate_up,
        name="input_send", flops=4 * flops,
    )
    other = lax.ppermute(send, "tensor", CORE_SWAP)
    keep = call(input_keep_kernel, out, pos, grads, w_gate_up, name="input_keep", flops=4 * flops)
    parts = call(add_kernel, out, keep, other, name="add")
    parts = lax.all_to_all(parts, "tensor", 0, 0, axis_index_groups=X_GROUPS, tiled=True)
    parts = call(x_sum_kernel, shaped((N_Y * 24, QUARTER)), parts, name="x_sum", flops=35 * 10**8).reshape(N_Y, 24, QUARTER)
    parts = lax.all_to_all(parts, ("dp", "tensor"), 0, 0, axis_index_groups=Z_GROUPS, tiled=True)
    input_grad = call(input_sum_kernel, shaped((6, D)), parts, name="input_sum")
    down_log_grad = down_grad.astype(f32) * down_w
    return input_grad, down_log_grad


def solution(mesh):
    in_specs = (P("dp", "tensor"),) * 5
    out_specs = (P(("dp", "tensor"), None), P("dp", "tensor"))
    return jax.shard_map(on_device, mesh=mesh, in_specs=in_specs, out_specs=out_specs, check_vma=False)
```

```python
import math

import jax
import jax.numpy as jnp
from jax import lax
from jax.experimental import pallas as pl
from jax.experimental.pallas import tpu as pltpu
from jax.sharding import PartitionSpec as P

D = 5120
FF_W = 8192
N_Z, N_Y, N_X, N_ZL = 2, 8, 4, 4
N_T = N_X * N_ZL * 2
TOK = 192
FEAT = 160
HALF_FEAT = 80
ROWS = 320
COLS = 256
HALF = D // 2
QUARTER = HALF // 4

coef_one = 0.6931472
coef_two = 0.2402265
coef_three = 0.0555041

NN = (((1,), (0,)), ((), ()))
NT = (((1,), (1,)), ((), ()))


def _turn_pairs(step):
    pairs = []
    for z in range(N_Z):
        for y in range(N_Y):
            for t in range(N_T):
                x1, rest = t // 16, (t % 16) ^ (2 * step)
                pairs.append(((z * N_Y + y) * N_T + t, (x1 * N_Y + y) * N_T + (1 - z) * 16 + rest))
    return pairs


TURNS = [_turn_pairs(step) for step in range(N_ZL)]
Z_SWAP = [(d, (d + N_Y) % (N_Z * N_Y)) for d in range(N_Z * N_Y)]
CORE_SWAP = [(t, t ^ 1) for t in range(N_T)]
ZL_GROUPS = [[x * 8 + zl * 2 + c for zl in range(N_ZL)] for x in range(N_X) for c in range(2)]
X_GROUPS = [[x * 8 + i for x in range(N_X)] for i in range(8)]
Y_GROUPS = [[z * N_Y + y for y in range(N_Y)] for z in range(N_Z)]
Z_GROUPS = [
    [(z * N_Y + y) * N_T + x * 8 + zl * 2 + c for z in range(N_Z) for zl in range(N_ZL)]
    for y in range(N_Y)
    for x in range(N_X)
    for c in range(2)
]


def decode(packed, fan):
    frac = ((packed >> 1) & 7).astype(jnp.float32) * 0.125
    power = jnp.where((packed & 16) != 0, 0.5, 1.0)
    power = power * jnp.where((packed & 32) != 0, 0.25, 1.0)
    power = power * jnp.where((packed & 64) != 0, 0.0625, 1.0)
    poly = 1.0 - frac * (coef_one - frac * (coef_two - coef_three * frac))
    value = power * poly * (3.0 / math.sqrt(fan))
    return jnp.where((packed & 1) != 0, -value, value)


def decode_kernel(gate_ref, up_ref, down_ref, out_ref, codes, values, in_sems, out_sems):
    pieces = [(i, core) for i in range(3) for core in range(2)]
    reads, writes = [], []
    for n, (i, core) in enumerate(pieces):
        ref = (gate_ref, up_ref, down_ref)[i].at[core * FEAT : (core + 1) * FEAT]
        reads.append(pltpu.make_async_copy(ref, codes.at[n], in_sems.at[n]))
        writes.append(
            pltpu.make_async_copy(values.at[n], out_ref.at[core, :, i * COLS : (i + 1) * COLS], out_sems.at[n])
        )
        reads[n].start()
    for n, (i, core) in enumerate(pieces):
        reads[n].wait()
        values[n] = decode(codes[n], (D, D, FF_W)[i]).astype(jnp.bfloat16)
        writes[n].start()
    for write in writes:
        write.wait()


def decode_down_kernel(codes_ref, out_ref):
    out_ref[...] = decode(codes_ref[...], FF_W)


def fetch(w_ref, which, cols, w, sems):
    copies = [pltpu.make_async_copy(w_ref.at[y, which, :, cols], w.at[y], sems.at[y]) for y in range(N_Y)]
    for copy in copies:
        copy.start()
    return copies


def fetch_acts(acts_ref, kind, acts, sems):
    rows = slice(kind * HALF_FEAT, (kind + 1) * HALF_FEAT)
    copies = [pltpu.make_async_copy(acts_ref.at[x, :, rows], acts.at[x], sems.at[x]) for x in range(N_X)]
    for copy in copies:
        copy.start()
    return copies


def block(acts_ref, x, my_zl, row):
    return jnp.concatenate([acts_ref[x, zl ^ my_zl, row : row + HALF_FEAT] for zl in range(N_ZL)], axis=0)


def forward(acts_ref, my_zl, row, w, ready):
    sums = [None, None]
    for x0 in range(2):
        ready(x0)
        acts = [block(acts_ref, 2 - 2 * h + x0, my_zl, row).T for h in range(2)]
        for half in range(2):
            rows = slice(half * HALF_FEAT, (half + 1) * HALF_FEAT)
            weights = jnp.concatenate([w(x0 * N_ZL + zl, rows) for zl in range(N_ZL)], axis=0)
            for h in range(2):
                part = acts[h][half * TOK : (half + 1) * TOK]
                part = lax.dot_general(part, weights, NN, preferred_element_type=jnp.float32)
                sums[h] = part if sums[h] is None else sums[h] + part
    return sums


GATE_UP, HIDDEN_GRAD = slice(0, 2 * COLS), slice(2 * COLS, 3 * COLS)


def near_kernel(pos_ref, acts_ref, w_ref, out_ref, w_far_ref, w, sems):
    core = pos_ref[1]
    copies = fetch(w_ref, core, GATE_UP, w, sems.at[0])
    others = fetch(w_ref, 1 - core, GATE_UP, w_far_ref, sems.at[1])

    def ready(x0):
        for copy in copies[x0 * N_ZL : (x0 + 1) * N_ZL]:
            copy.wait()

    for h, total in enumerate(forward(acts_ref, pos_ref[3], 0, lambda y, rows: w[y, rows], ready)):
        out_ref[h] = total
    for copy in others:
        copy.wait()


def gate_up_kernel(pos_ref, acts_ref, near_ref, w_far_ref, own_ref, send_ref, acts, sems):
    copies = fetch_acts(acts_ref, 0, acts, sems)

    def ready(x0):
        copies[x0].wait()
        copies[2 + x0].wait()

    for h, total in enumerate(forward(acts, pos_ref[3], 0, lambda y, rows: w_far_ref[y, rows], ready)):
        total += near_ref[h]
        own_ref[h] = total
        send_ref[h] = total.astype(jnp.bfloat16)


def hidden_grad_kernel(pos_ref, near_ref, far_ref, w_ref, own_ref, send_ref, grads_ref, acts, sems):
    core, my_zl = pos_ref[1], pos_ref[3]
    copies = fetch_acts(far_ref, 1, acts, sems)
    totals = forward(near_ref, my_zl, HALF_FEAT, lambda y, rows: w_ref[y, core, rows, HIDDEN_GRAD], lambda x0: None)
    for copy in copies:
        copy.wait()
    far = forward(acts, my_zl, 0, lambda y, rows: w_ref[y, 1 - core, rows, HIDDEN_GRAD], lambda x0: None)
    for h in range(2):
        total = totals[h] + far[h]
        own_ref[h] = total
        send_ref[h] = total.astype(jnp.bfloat16)
    for side, (ref, row) in enumerate(((near_ref, HALF_FEAT), (acts, 0))):
        for x0 in range(2):
            for h in range(2):
                grads_ref[side, x0, :, h * 2 * TOK : (h + 1) * 2 * TOK] = block(ref, 2 - 2 * h + x0, my_zl, row)


def copy_kernel(w_ref, out_ref):
    out_ref[...] = w_ref[:, :, :, : 2 * COLS]


def down_kernel(pos_ref, grads_ref, own_ref, got_ref, out_ref):
    core = pos_ref[1]
    blank = jnp.zeros((TOK, COLS), jnp.bfloat16)
    rows = []
    for h in range(2):
        total = own_ref[h] + got_ref[h].astype(jnp.float32)
        gate, up = total[:, :COLS], total[:, COLS:]
        hidden = (gate * jax.nn.sigmoid(gate) * up).astype(jnp.bfloat16)
        rows += [jnp.concatenate([hidden, blank], axis=1), jnp.concatenate([blank, hidden], axis=1)]
    hidden = jnp.concatenate(rows, axis=0)
    for x0 in range(2):
        for side, which in ((0, core), (1, 1 - core)):
            acts = grads_ref[side, x0]
            part = lax.dot_general(acts, hidden, NN, preferred_element_type=jnp.float32).astype(jnp.bfloat16)
            for zl in range(N_ZL):
                rows = part[zl * HALF_FEAT : (zl + 1) * HALF_FEAT]
                out_ref[x0 * N_ZL + zl, which, :HALF_FEAT] = rows[:, :COLS]
                out_ref[x0 * N_ZL + zl, which, HALF_FEAT:] = rows[:, COLS:]


def input_part(pos_ref, own_ref, got_ref, own_hg_ref, got_hg_ref, w_ref, out_ref, side):
    rows = N_X * 48
    row = lax.broadcasted_iota(jnp.int32, (rows, 2 * TOK), 0)
    col = lax.broadcasted_iota(jnp.int32, (rows, 2 * TOK), 1)
    x = (row * 1366) >> 16
    left = row - 48 * x
    h = jnp.where(left >= 24, 1, 0)
    left = left - 24 * h
    zl = (left * 10923) >> 16
    wanted = h * TOK + x * 48 + zl * 12 + side * 6 + left - 6 * zl
    pick = jnp.where(wanted == col, 1.0, 0.0).astype(jnp.bfloat16)
    grads = []
    for h in range(2):
        total = own_ref[h] + got_ref[h].astype(jnp.float32)
        gate, up = total[:, :COLS], total[:, COLS:]
        hidden_grad = own_hg_ref[h] + got_hg_ref[h].astype(jnp.float32)
        sig = jax.nn.sigmoid(gate)
        gate_grad = (hidden_grad * up * sig * (1.0 + gate * (1.0 - sig))).astype(jnp.bfloat16)
        up_grad = (hidden_grad * gate * sig).astype(jnp.bfloat16)
        grads.append(jnp.concatenate([gate_grad, up_grad], axis=1))
    grads = jnp.concatenate(grads, axis=0)
    grads = lax.dot_general(pick, grads, NN, preferred_element_type=jnp.float32).astype(jnp.bfloat16)
    for q in range(4):
        pair = w_ref[2 * q : 2 * q + 2].reshape(2 * ROWS, 2 * COLS)
        part = lax.dot_general(grads, pair, NT, preferred_element_type=jnp.float32)
        at = slice(q * 2 * ROWS, (q + 1) * 2 * ROWS)
        out_ref[:, :, at] = part.astype(jnp.bfloat16).reshape(N_X, 48, 2 * ROWS)


def input_send_kernel(pos_ref, *refs):
    input_part(pos_ref, *refs, 1 - pos_ref[1])


def input_keep_kernel(pos_ref, *refs):
    input_part(pos_ref, *refs, pos_ref[1])


def add_kernel(a_ref, b_ref, out_ref):
    out_ref[...] = (a_ref[...].astype(jnp.float32) + b_ref[...].astype(jnp.float32)).astype(jnp.bfloat16)


def x_sum_kernel(parts_ref, out_ref):
    total = parts_ref[0].astype(jnp.float32)
    for i in range(1, N_X):
        total += parts_ref[i].astype(jnp.float32)
    total = total.astype(jnp.bfloat16)
    row = lax.broadcasted_iota(jnp.int32, (N_Y * 24, 48), 0)
    col = lax.broadcasted_iota(jnp.int32, (N_Y * 24, 48), 1)
    k = (row * 2731) >> 16
    left = row - 24 * k
    packed = None
    for q in range(4):
        inside = (left >= 6 * q) & (left < 6 * q + 6)
        pick = jnp.where(inside & (k * 6 + left - 6 * q == col), 1.0, 0.0).astype(jnp.bfloat16)
        part = total[:, q * QUARTER : (q + 1) * QUARTER]
        part = lax.dot_general(pick, part, NN, preferred_element_type=jnp.float32)
        packed = part if packed is None else packed + part
    out_ref[...] = packed.astype(jnp.bfloat16)


def input_sum_kernel(parts_ref, out_ref):
    row = lax.broadcasted_iota(jnp.int32, (8, 24), 0)
    col = lax.broadcasted_iota(jnp.int32, (8, 24), 1)
    for z in range(2):
        total = parts_ref[4 * z].astype(jnp.float32)
        for i in range(1, 4):
            total += parts_ref[4 * z + i].astype(jnp.float32)
        total = total.astype(jnp.bfloat16)
        for q in range(4):
            pick = jnp.where((row + 6 * q == col) & (row < 6), 1.0, 0.0).astype(jnp.bfloat16)
            part = lax.dot_general(pick, total, NN, preferred_element_type=jnp.float32)
            at = z * HALF + q * QUARTER
            out_ref[:, at : at + QUARTER] = part[:6].astype(jnp.bfloat16)


VMEM = pl.BlockSpec(memory_space=pltpu.VMEM)
SMEM = pl.BlockSpec(memory_space=pltpu.SMEM)
HBM = pl.BlockSpec(memory_space=pltpu.HBM)


def call(kernel, out_shapes, *args, name, flops=0, scratch=(), hbm=(), limit=16, out_spec=VMEM):
    specs = [SMEM if a.dtype == jnp.int32 and a.ndim == 1 else HBM if i in hbm else VMEM for i, a in enumerate(args)]
    moved = 0
    if flops:
        moved = sum(a.size * a.dtype.itemsize for a in args)
        moved += sum(o.size * o.dtype.itemsize for o in jax.tree.leaves(out_shapes))
    return pl.pallas_call(
        kernel,
        out_shape=out_shapes,
        in_specs=specs,
        out_specs=jax.tree.map(lambda _: out_spec, out_shapes),
        scratch_shapes=scratch,
        compiler_params=pltpu.CompilerParams(vmem_limit_bytes=limit * 2**20),
        cost_estimate=pl.CostEstimate(flops=flops, bytes_accessed=moved, transcendentals=0),
        name=name,
    )(*args)


def shaped(shape, dtype=jnp.bfloat16):
    return jax.ShapeDtypeStruct(shape, dtype)


def on_device(inputs, grad_out, gate_codes, up_codes, down_codes):
    dp, tensor = lax.axis_index("dp"), lax.axis_index("tensor")
    pos = jnp.stack([dp // N_Y, tensor % 2, dp % N_Y, tensor // 2 % N_ZL]).astype(jnp.int32)
    wide, bf16, f32 = 3 * COLS, jnp.bfloat16, jnp.float32

    w = call(
        decode_kernel, shaped((2, FEAT, wide)), gate_codes, up_codes, down_codes,
        name="decode", flops=ROWS * COLS * 32,
        scratch=[
            pltpu.VMEM((6, FEAT, COLS), jnp.int32), pltpu.VMEM((6, FEAT, COLS), bf16),
            pltpu.SemaphoreType.DMA((6,)), pltpu.SemaphoreType.DMA((6,)),
        ],
        hbm=(0, 1, 2), limit=60, out_spec=HBM,
    )
    w = lax.all_gather(w, "dp", axis=0, axis_index_groups=Y_GROUPS)

    def folded(acts):
        acts = acts.T
        return jnp.concatenate([acts[:HALF_FEAT], acts[HALF_FEAT:]], axis=1)

    acts = jnp.concatenate([folded(inputs), folded(grad_out)], axis=0)
    acts = jnp.stack([lax.ppermute(acts, ("dp", "tensor"), turn) for turn in TURNS])
    acts = jnp.broadcast_to(acts[None], (N_X, N_ZL, FEAT, 2 * TOK))
    near = lax.all_to_all(acts, "tensor", 0, 0, axis_index_groups=X_GROUPS, tiled=True)
    far = lax.ppermute(near, "tensor", CORE_SWAP)

    flops = HALF * COLS * 2 * TOK
    gate_up_shape, hidden_grad_shape = (2, TOK, 2 * COLS), (2, TOK, COLS)
    w_shape = (N_Y, FEAT, 2 * COLS)
    acts_space = [pltpu.VMEM((N_X, N_ZL, HALF_FEAT, 2 * TOK), bf16), pltpu.SemaphoreType.DMA((N_X,))]
    gate_up, w_far = call(
        near_kernel, (shaped(gate_up_shape, f32), shaped(w_shape)), pos, near, w, name="forward_near", flops=2 * flops,
        hbm=(2,), limit=50, scratch=[pltpu.VMEM(w_shape, bf16), pltpu.SemaphoreType.DMA((2, N_Y))],
    )
    own, send = call(
        gate_up_kernel, (shaped(gate_up_shape, f32), shaped(gate_up_shape)), pos, far, gate_up, w_far, name="gate_up",
        hbm=(1,), scratch=acts_space,
    )
    got = lax.ppermute(send, "dp", Z_SWAP)
    own_hg, send, grads = call(
        hidden_grad_kernel,
        (shaped(hidden_grad_shape, f32), shaped(hidden_grad_shape), shaped((2, 2, N_ZL * HALF_FEAT, 4 * TOK))),
        pos, near, far, w, name="hidden_grad", hbm=(2,), scratch=acts_space,
    )
    w_own, codes, _ = lax.optimization_barrier((w, down_codes, own_hg))
    down_w = call(decode_down_kernel, shaped((ROWS, COLS), f32), codes, name="decode_down", flops=ROWS * COLS * 32)
    send, down_w = lax.optimization_barrier((send, down_w))
    got_hg = lax.ppermute(send, "dp", Z_SWAP)
    w_gate_up = call(copy_kernel, shaped((N_Y, 2, FEAT, 2 * COLS)), w_own, name="copy", flops=flops)

    got, own_hg = lax.optimization_barrier((got, own_hg))
    down = call(down_kernel, shaped((N_Y, 2, FEAT, COLS)), pos, grads, own, got, name="down")
    down_grad = lax.psum_scatter(
        down.reshape(N_Y * ROWS, COLS), "dp", scatter_dimension=0, axis_index_groups=Y_GROUPS, tiled=True
    )
    down, got_hg, w_gate_up, down_w = lax.optimization_barrier((down, got_hg, w_gate_up, down_w))

    out = shaped((N_X, 48, HALF))
    grads = (own, got, own_hg, got_hg)
    send = call(input_send_kernel, out, pos, *grads, w_gate_up, name="input_send", flops=flops)
    other = lax.ppermute(send, "tensor", CORE_SWAP)
    keep = call(input_keep_kernel, out, pos, *grads, w_gate_up, name="input_keep", flops=flops)
    parts = call(add_kernel, out, keep, other, name="add")
    parts = lax.all_to_all(parts, "tensor", 0, 0, axis_index_groups=X_GROUPS, tiled=True)
    parts = call(x_sum_kernel, shaped((N_Y * 24, QUARTER)), parts, name="x_sum", flops=35 * 10**8).reshape(N_Y, 24, QUARTER)
    parts = lax.all_to_all(parts, ("dp", "tensor"), 0, 0, axis_index_groups=Z_GROUPS, tiled=True)
    input_grad = call(input_sum_kernel, shaped((6, D)), parts, name="input_sum")
    down_log_grad = down_grad.astype(f32) * down_w
    return input_grad, down_log_grad


def solution(mesh):
    in_specs = (P("dp", "tensor"),) * 5
    out_specs = (P(("dp", "tensor"), None), P("dp", "tensor"))
    return jax.shard_map(on_device, mesh=mesh, in_specs=in_specs, out_specs=out_specs, check_vma=False)
```
